256 devices in a mesh: gx: 16 (over y, z_lo), gy: 16 (over z_hi, x, core).
Axes of the slice: x: 4, y: 4, z: 8 (z_hi: 2, z_lo: 4; z = z_hi * 4 + z_lo), core: 2. Of those that a mesh axis runs over, the one named last changes fastest.
Arguments:
- latents: bfloat16 [16, 16, 512, 128], P('gx', 'gy'), may hold values from -6 to 6
- edge_latents: bfloat16 [16, 16, 4096, 128], P('gx', 'gy'), may hold values from -6 to 6
- senders: int32 [16, 16, 4096], P('gx', 'gy'), may hold values from 0 to 1663, as said below
- receivers: int32 [16, 16, 4096], P('gx', 'gy'), may hold values from 0 to 255
- ghost_rows: int32 [16, 16, 3, 3, 128], P('gx', 'gy'), may hold values from 0 to 511
- edge_count: int32 [16, 16], P('gx', 'gy'), may hold values from 1024 to 4096, as said below
- node_cotangent: bfloat16 [16, 16, 512, 128], P('gx', 'gy'), may hold values from -6 to 6
- edge_cotangent: bfloat16 [16, 16, 4096, 128], P('gx', 'gy'), may hold values from -6 to 6
- edge_first: bfloat16 [2, 384, 128], replicated, may hold values from -0.3125 to 0.3125
- edge_second: bfloat16 [2, 128, 128], replicated, may hold values from -0.5 to 0.5
- edge_scale: float32 [2, 128], replicated, may hold values from 0.5 to 1.5
- node_first: bfloat16 [2, 256, 128], replicated, may hold values from -0.375 to 0.375
- node_second: bfloat16 [2, 128, 128], replicated, may hold values from -0.5 to 0.5
- node_scale: float32 [2, 128], replicated, may hold values from 0.5 to 1.5
Outputs:
- nodes_out: bfloat16 [16, 16, 512, 128], P('gx', 'gy')
- edges_out: bfloat16 [16, 16, 4096, 128], P('gx', 'gy')
- latents_grad: float32 [16, 16, 512, 128], P('gx', 'gy')
- edge_latents_grad: float32 [16, 16, 4096, 128], P('gx', 'gy')
- edge_first_grad: float32 [2, 384, 128], replicated
- edge_second_grad: float32 [2, 128, 128], replicated
- edge_scale_grad: float32 [2, 128], replicated
- node_first_grad: float32 [2, 256, 128], replicated
- node_second_grad: float32 [2, 128, 128], replicated
- node_scale_grad: float32 [2, 128], replicated
The draws below stay inside these ranges and needn't reach their ends.
Inputs may be any that keep to these rules, and one draw needn't show every extreme that they name: `senders`: rows 0 to 511 of the node table are the domain's particles; row 512 + k * 128 + j is ghost row j of slot k = 3 a + b, from the neighbour at offset (a - 1, b - 1); slot 4 is never named. `edge_count`: edge slots at positions below the count are live, later ones are padding.
All inputs are finite; a program needn't handle non-finite values.
Results may differ from the reference program's by a relative error of at most 0.02.
Values may be sent and summed in bfloat16 or wider, within the bound.
No kernel may reach another device: no remote copies, remote signals or barrier semaphores. Data moves between devices by JAX's collectives and lax.ppermute only.
A program may use at most 128 MiB of HBM per device.

```python
import jax
import jax.numpy as jnp
from jax import lax

L = 128
H = 128
LAYERS = 2
TILE = 256
DEG = 8
P_SIZE = 512
G = 128
E = 4096
GRID_X = 16
GRID_Y = 16


def draw_senders(key, part):
    key = jax.random.fold_in(key, 11)
    keys = jax.random.split(key, 4)
    layout_shape = (GRID_X, GRID_Y, E)
    choose = jax.random.randint(keys[0], layout_shape, 0, 10)
    local_rows = jax.random.randint(keys[1], layout_shape, 0, P_SIZE)
    direction = jax.random.randint(keys[2], layout_shape, 0, 8)
    direction = direction + (direction >= 4).astype(jnp.int32)
    position = jax.random.randint(keys[3], layout_shape, 0, G)
    result = jnp.where(choose < 3, P_SIZE + direction * G + position, local_rows)
    return result.at[0, 0, 0].set(P_SIZE + 9 * G - 1).astype(jnp.int32)


def draw_edge_count(key, part):
    key = jax.random.fold_in(key, 23)
    counts = E // 4 + jax.random.randint(key, (GRID_X, GRID_Y), 0, E - E // 4 + 1)
    return counts.at[0, 0].set(E).astype(jnp.int32)


def place_ends(values, key, least, top_value):
    longest = values.shape.index(max(values.shape))
    spots = []
    for shift in (0, 1):
        where = [jax.random.randint(jax.random.fold_in(key, axis), (), 0, length) for axis, length in enumerate(values.shape)]
        where[longest] = (where[longest] + shift) % values.shape[longest]
        spots.append(tuple(where))
    return values.at[spots[0]].set(least).at[spots[1]].set(top_value)


def levels(rng, extent, shards, low, high):
    def one(axis_at, shards_of):
        heights = jax.random.uniform(jax.random.fold_in(jax.random.fold_in(rng, 6), axis_at), (shards_of,), jnp.float32, low / len(shards), high / len(shards))
        return jnp.repeat(jnp.exp(heights), extent[axis_at] // shards_of).reshape((-1,) + (1,) * (len(extent) - axis_at - 1))

    level = one(*shards[0])
    for cut in shards[1:]:
        level = level * one(*cut)
    return level


def noise(own_key, dims, scale, bound, cuts=(), kind=jnp.bfloat16):
    gain = levels(own_key, dims, cuts, -0.22, 0.18) if cuts else 1.0
    array = jax.random.normal(own_key, dims, jnp.float32) * scale * gain
    return jnp.minimum(jnp.maximum(array, -bound), bound).astype(kind)


def setup_inputs(seed: int = 0) -> dict:
    streams_of = jax.random.split(jax.random.key(seed), 15)
    latents = noise(streams_of[0], (GRID_X, GRID_Y, P_SIZE, L), 1.0, 6.0, ((0, 16), (1, 16)))
    edge_latents = noise(streams_of[1], (GRID_X, GRID_Y, E, L), 1.0, 6.0, ((0, 16), (1, 16)))
    senders = draw_senders(jax.random.fold_in(streams_of[14], 71), 0)
    receivers = place_ends(jax.random.randint(streams_of[3], (GRID_X, GRID_Y, E), 0, TILE), jax.random.fold_in(streams_of[3], 1), 0, TILE - 1).astype(jnp.int32)
    ghost_rows = place_ends(jax.random.randint(streams_of[4], (GRID_X, GRID_Y, 3, 3, G), 0, P_SIZE), jax.random.fold_in(streams_of[4], 1), 0, P_SIZE - 1).astype(jnp.int32)
    edge_count = draw_edge_count(jax.random.fold_in(streams_of[14], 71), 0)
    node_cotangent = noise(streams_of[6], (GRID_X, GRID_Y, P_SIZE, L), 1.0, 6.0, ((0, 16), (1, 16)))
    edge_cotangent = noise(streams_of[7], (GRID_X, GRID_Y, E, L), 1.0, 6.0, ((0, 16), (1, 16)))
    edge_first = noise(streams_of[8], (LAYERS, 3 * L, H), (3 * L) ** -0.5, 0.3125)
    edge_second = noise(streams_of[9], (LAYERS, H, L), H ** -0.5, 0.5)
    edge_scale = jnp.clip(1.0 + 0.1 * jax.random.normal(streams_of[10], (LAYERS, L), jnp.float32), 0.5, 1.5)
    node_first = noise(streams_of[11], (LAYERS, 2 * L, H), (2 * L) ** -0.5, 0.375)
    node_second = noise(streams_of[12], (LAYERS, H, L), H ** -0.5, 0.5)
    node_scale = jnp.clip(1.0 + 0.1 * jax.random.normal(streams_of[13], (LAYERS, L), jnp.float32), 0.5, 1.5)
    return dict(latents=latents, edge_latents=edge_latents, senders=senders, receivers=receivers, ghost_rows=ghost_rows, edge_count=edge_count, node_cotangent=node_cotangent, edge_cotangent=edge_cotangent, edge_first=edge_first, edge_second=edge_second, edge_scale=edge_scale, node_first=node_first, node_second=node_second, node_scale=node_scale)


epsilon = 1e-05

def normalize(values, gains):
    center = lax.optimization_barrier(jnp.mean(values, axis=-1, keepdims=True))
    spread = lax.optimization_barrier(jnp.mean(jnp.square(values - center), axis=-1, keepdims=True))
    return (values - center) * lax.rsqrt(spread + epsilon) * gains

def layer_update(node32, ghost32, edge32, sender_ids, receiver_ids, edge_total, params):
    edge_first, edge_second, edge_scale, node_first, node_second, node_scale = params
    blocks = sender_ids.shape[0] // TILE
    node_table = jnp.concatenate([node32, ghost32.reshape(-1, L)], axis=0)
    sender_rows = jnp.take(node_table, sender_ids, axis=0).astype(jnp.bfloat16)
    onehot = (receiver_ids.reshape(blocks, TILE)[:, :, None] == jnp.arange(TILE, dtype=jnp.int32)[None, None, :]).astype(jnp.float32)
    tile_rows = jnp.repeat(node32.reshape(-1, TILE, L), DEG, axis=0)
    received = jnp.einsum('bei,bil->bel', onehot, tile_rows, precision=lax.Precision.HIGHEST).reshape(-1, L).astype(jnp.bfloat16)
    joined = jnp.concatenate([sender_rows, received, edge32.astype(jnp.bfloat16)], axis=1)
    edge_hidden = jax.nn.silu(jnp.dot(joined, edge_first.astype(jnp.bfloat16), preferred_element_type=jnp.float32)).astype(jnp.bfloat16)
    live_mask = (jnp.arange(sender_ids.shape[0], dtype=jnp.int32) < edge_total).astype(jnp.float32)[:, None]
    message = normalize(jnp.dot(edge_hidden, edge_second.astype(jnp.bfloat16), preferred_element_type=jnp.float32), edge_scale) * live_mask
    edge_next = (edge32 + message).astype(jnp.bfloat16)
    message_b = message.astype(jnp.bfloat16)
    summed = jnp.einsum('bei,bel->bil', onehot, message_b.astype(jnp.float32).reshape(blocks, TILE, L), precision=lax.Precision.HIGHEST)
    inbound = summed.reshape(-1, DEG, TILE, L).sum(axis=1).reshape(-1, L).astype(jnp.bfloat16)
    node_input = jnp.concatenate([node32.astype(jnp.bfloat16), inbound], axis=1)
    node_hidden = jax.nn.silu(jnp.dot(node_input, node_first.astype(jnp.bfloat16), preferred_element_type=jnp.float32)).astype(jnp.bfloat16)
    update = normalize(jnp.dot(node_hidden, node_second.astype(jnp.bfloat16), preferred_element_type=jnp.float32), node_scale)
    node_next = (node32 + update).astype(jnp.bfloat16)
    return (node_next, edge_next)

def gather_ghosts(node32, ghost_rows):
    picked = jax.vmap(jax.vmap(lambda source, indices: jnp.take(source, indices, axis=0)))(node32, ghost_rows)
    outside = jnp.ones((3, 3), jnp.float32).at[1, 1].set(0.0)
    picked = picked * outside[:, :, None, None]
    flipped = picked[:, :, ::-1, ::-1]
    padded = jnp.pad(flipped, ((1, 1), (1, 1), (0, 0), (0, 0), (0, 0), (0, 0)))
    slot_rows = []
    for row_slot in range(3):
        columns = [padded[row_slot:row_slot + GRID_X, col_slot:col_slot + GRID_Y, row_slot, col_slot] for col_slot in range(3)]
        slot_rows.append(jnp.stack(columns, axis=2))
    return jnp.stack(slot_rows, axis=2)

def flatten_domains(values):
    return values.reshape((GRID_X * GRID_Y,) + values.shape[2:])

def reference(latents, edge_latents, senders, receivers, ghost_rows, edge_count, node_cotangent, edge_cotangent, edge_first, edge_second, edge_scale, node_first, node_second, node_scale):
    params32 = (edge_first.astype(jnp.float32), edge_second.astype(jnp.float32), edge_scale.astype(jnp.float32), node_first.astype(jnp.float32), node_second.astype(jnp.float32), node_scale.astype(jnp.float32))

    def forward(node32, edge32, params):
        nodes_b = latents
        edges_b = edge_latents
        for layer_index in range(LAYERS):
            ghosts = gather_ghosts(node32, ghost_rows)
            layer_params = tuple((weights[layer_index] for weights in params))

            def domain(packed):
                return layer_update(packed[0], packed[1], packed[2], packed[3], packed[4], packed[5], layer_params)
            node_next, edge_next = lax.map(jax.checkpoint(domain), (flatten_domains(node32), flatten_domains(ghosts), flatten_domains(edge32), flatten_domains(senders), flatten_domains(receivers), flatten_domains(edge_count)))
            nodes_b = node_next.reshape(node32.shape)
            edges_b = edge_next.reshape(edge32.shape)
            node32 = nodes_b.astype(jnp.float32)
            edge32 = edges_b.astype(jnp.float32)
        return (nodes_b, edges_b)
    outputs, pullback = jax.vjp(forward, latents.astype(jnp.float32), edge_latents.astype(jnp.float32), params32)
    latents_grad, edge_latents_grad, grads = pullback((node_cotangent, edge_cotangent))
    return (outputs[0], outputs[1], latents_grad, edge_latents_grad, grads[0], grads[1], grads[2], grads[3], grads[4], grads[5])
```

```python
import jax
import jax.numpy as jnp
from jax import lax
from jax.experimental import pallas as pl
from jax.experimental.pallas import tpu as pltpu
from jax.sharding import PartitionSpec as P

L = 128
LAYERS = 2
TILE = 256
DEG = 8
SLOTS = 8
G = 128
NODES = 512
EDGES = 4096
GHOSTS = SLOTS * G
HALF = (NODES + GHOSTS) // 2
BLOCK = 512
BLOCKS = EDGES // BLOCK
PER_TILE = TILE * DEG // BLOCK
PACKED = 1024

F32 = jnp.float32
BF16 = jnp.bfloat16
epsilon = 1e-05


def dot(a, b):
    return jnp.dot(a, b, preferred_element_type=F32)


def dot_nt(a, b):
    return lax.dot_general(a, b, (((1,), (1,)), ((), ())), preferred_element_type=F32)


def dot_tn(a, b):
    return lax.dot_general(a, b, (((0,), (0,)), ((), ())), preferred_element_type=F32)


def sigmoid(v):
    return 1.0 / (1.0 + jnp.exp(-v))


def column(rows, count):
    parts = [
        jnp.transpose(jnp.broadcast_to(rows[i : i + 1, :], (128, 128))) for i in range(count)
    ]
    return jnp.concatenate(parts, axis=0) if count > 1 else parts[0]


def flat_row(rows, count):
    parts = [rows[i : i + 1, :] for i in range(count)]
    return jnp.concatenate(parts, axis=1) if count > 1 else parts[0]


def hits(col, width):
    lane = lax.broadcasted_iota(jnp.int32, col.shape, 1).astype(F32)
    parts = [
        jnp.where(col == lane + float(128 * t), 1.0, 0.0).astype(BF16) for t in range(width // 128)
    ]
    return jnp.concatenate(parts, axis=1)


def hits_t(row, height):
    sub = lax.broadcasted_iota(jnp.int32, (height, row.shape[1]), 0).astype(F32)
    return jnp.where(sub == row, 1.0, 0.0).astype(BF16)


def layer_norm(y):
    center = y - jnp.mean(y, axis=-1, keepdims=True)
    spread = jnp.mean(center * center, axis=-1, keepdims=True)
    rstd = lax.rsqrt(spread + epsilon)
    return center * rstd, rstd


def layer_norm_grad(dn, n, rstd):
    return rstd * (
        dn
        - jnp.mean(dn, axis=-1, keepdims=True)
        - n * jnp.mean(dn * n, axis=-1, keepdims=True)
    )


def silu_grad(z):
    s = sigmoid(z)
    return s * (1.0 + z * (1.0 - s))


def pick(nodes_b, ghost_row_ref, out_ref):
    for s in range(SLOTS):
        col = column(ghost_row_ref[s : s + 1, :], 1)
        out_ref[pl.ds(s * G, G), :] = dot(hits(col, NODES), nodes_b).astype(BF16)


def build_table(nodes_ref, ghosts_ref, table):
    table[0:NODES, 0:L] = nodes_ref[...]
    table[NODES:HALF, 0:L] = ghosts_ref[0 : HALF - NODES, :]
    table[:, L : 2 * L] = ghosts_ref[HALF - NODES :, :]


def block_rows(ref, b):
    count = BLOCK // 128
    return ref[pl.ds(b * count, count), :]


def send_gather(b, srow_ref, table):
    col = column(block_rows(srow_ref, b), BLOCK // 128)
    upper = col >= float(HALF)
    both = dot(hits(jnp.where(upper, col - float(HALF), col), HALF), table[...])
    return jnp.where(upper, both[:, L:], both[:, :L]).astype(BF16)


def receive_hits(b, rrow_ref):
    return hits(column(block_rows(rrow_ref, b), BLOCK // 128), TILE)


def tile_of(b):
    return pl.ds(pl.multiple_of((b // PER_TILE) * TILE, TILE), TILE)


def block_of(b):
    return pl.ds(pl.multiple_of(b * BLOCK, BLOCK), BLOCK)


def live_of(b, count):
    slot = lax.broadcasted_iota(jnp.int32, (BLOCK, L), 0) + b * BLOCK
    return jnp.where(slot < count, 1.0, 0.0)


def edge_hidden(sent, received, edges_b, w1_ref):
    joined = jnp.concatenate([sent, received, edges_b], axis=1)
    return joined, dot(joined, w1_ref[...])


def edges_forward(
    b, count, table, nodes_ref, edges_ref, srow_ref, rrow_ref, w1_ref, w2_ref, g1_ref, inbound
):
    sent = send_gather(b, srow_ref, table)
    received = dot(receive_hits(b, rrow_ref), nodes_ref[tile_of(b), :]).astype(BF16)
    edges_b = edges_ref[block_of(b), :]
    joined, z = edge_hidden(sent, received, edges_b, w1_ref)
    hidden = (z * sigmoid(z)).astype(BF16)
    n, rstd = layer_norm(dot(hidden, w2_ref[...]))
    message = n * g1_ref[...] * live_of(b, count)
    edges_next = (edges_b.astype(F32) + message).astype(BF16)
    back = hits_t(flat_row(block_rows(rrow_ref, b), BLOCK // 128), TILE)
    inbound[tile_of(b), :] += dot(back, message.astype(BF16))
    return sent, joined, z, hidden, n, rstd, edges_next


def nodes_forward(nodes_b, inbound_b, u1_ref, u2_ref, g2_ref):
    joined = jnp.concatenate([nodes_b, inbound_b], axis=1)
    z = dot(joined, u1_ref[...])
    hidden = (z * sigmoid(z)).astype(BF16)
    n, rstd = layer_norm(dot(hidden, u2_ref[...]))
    nodes_next = (nodes_b.astype(F32) + n * g2_ref[...]).astype(BF16)
    return joined, z, hidden, n, rstd, nodes_next


def nodes_backward(grad, joined, z, hidden, n, rstd, u1_ref, u2_ref, g2_ref, sums):
    sums[897:898, :] = jnp.sum(grad * n, axis=0, keepdims=True)
    dy = layer_norm_grad(grad * g2_ref[...], n, rstd).astype(BF16)
    sums[768:896, :] = dot_tn(hidden, dy)
    dz = (dot_nt(dy, u2_ref[...]).astype(BF16).astype(F32) * silu_grad(z)).astype(BF16)
    sums[512:768, :] = dot_tn(joined, dz)
    back = dot_nt(dz, u1_ref[...]).astype(BF16)
    return back[:, :L].astype(F32), back[:, L:]


def edges_backward(
    b, count, joined, z, hidden, n, rstd, grad_ref, dinbound, srow_ref, rrow_ref, w1_ref, w2_ref,
    g1_ref, sums, dnodes, dtable
):
    grad = grad_ref[block_of(b), :].astype(F32)
    from_nodes = dot(receive_hits(b, rrow_ref), dinbound[tile_of(b), :])
    dmessage = (grad + from_nodes) * live_of(b, count)
    sums[896:897, :] += jnp.sum(dmessage * n, axis=0, keepdims=True)
    dy = layer_norm_grad(dmessage * g1_ref[...], n, rstd).astype(BF16)
    sums[384:512, :] += dot_tn(hidden, dy)
    dz = (dot_nt(dy, w2_ref[...]).astype(BF16).astype(F32) * silu_grad(z)).astype(BF16)
    sums[0:384, :] += dot_tn(joined, dz)
    back = dot_nt(dz, w1_ref[...]).astype(BF16)
    dsent, dreceived, dedges = (back[:, :L], back[:, L : 2 * L], back[:, 2 * L :])
    row = flat_row(block_rows(srow_ref, b), BLOCK // 128)
    col = column(block_rows(srow_ref, b), BLOCK // 128)
    upper = col >= float(HALF)
    zero = jnp.zeros_like(dsent)
    dsent32 = dsent.astype(F32)
    pair = jnp.concatenate(
        [jnp.where(upper, 0.0, dsent32).astype(BF16), jnp.where(upper, dsent32, 0.0).astype(BF16)],
        axis=1,
    )
    dtable[...] += dot(hits_t(jnp.where(row >= float(HALF), row - float(HALF), row), HALF), pair)
    back_hits = hits_t(flat_row(block_rows(rrow_ref, b), BLOCK // 128), TILE)
    dnodes[tile_of(b), :] += dot(back_hits, dreceived)
    return grad + dedges.astype(F32)


def pack(sums, out_ref):
    gains = sums[896:898, :]
    sums[898:900, :] = gains - gains.astype(BF16).astype(F32)
    out_ref[...] = sums[...].astype(BF16)


def ghost_grads(dtable, out_ref):
    out_ref[0 : HALF - NODES, :] = dtable[NODES:HALF, 0:L].astype(BF16)
    out_ref[HALF - NODES :, :] = dtable[:, L : 2 * L].astype(BF16)


def add_returned(partial, returned_ref, ghost_row_ref):
    row = flat_row(ghost_row_ref[...], SLOTS)
    return partial + dot(hits_t(row, NODES), returned_ref[...])


def pick_kernel(nodes_ref, ghost_row_ref, picked_ref):
    pick(nodes_ref[...], ghost_row_ref, picked_ref)


def first_kernel(
    count_ref, nodes_ref, ghosts_ref, edges_ref, srow_ref, rrow_ref, ghost_row_ref, w1_ref, w2_ref,
    g1_ref, u1_ref, u2_ref, g2_ref, nodes_out, edges_out, sent_out, inbound_out, picked_out, table,
    inbound
):
    count = count_ref[0, 0]
    build_table(nodes_ref, ghosts_ref, table)
    inbound[...] = jnp.zeros_like(inbound)

    def step(b, carry):
        sent, _, _, _, _, _, edges_next = edges_forward(
            b, count, table, nodes_ref, edges_ref, srow_ref, rrow_ref, w1_ref, w2_ref, g1_ref,
            inbound
        )
        sent_out[block_of(b), :] = sent
        edges_out[block_of(b), :] = edges_next
        return carry

    lax.fori_loop(0, BLOCKS, step, 0)
    inbound_b = inbound[...].astype(BF16)
    inbound_out[...] = inbound_b
    nodes_next = nodes_forward(nodes_ref[...], inbound_b, u1_ref, u2_ref, g2_ref)[-1]
    nodes_out[...] = nodes_next
    pick(nodes_next, ghost_row_ref, picked_out)


def middle_kernel(
    count_ref, nodes_ref, ghosts_ref, edges_ref, srow_ref, rrow_ref, w1_ref, w2_ref, g1_ref, u1_ref,
    u2_ref, g2_ref, node_grad_ref, edge_grad_ref, nodes_out, edges_out, ghost_grad_out,
    edge_grad_out, node_grad_out, packed_out, table, inbound, joined_all, z_all, hidden_all, n_all,
    rstd_all, dinbound, dtable, sums
):
    count = count_ref[0, 0]
    build_table(nodes_ref, ghosts_ref, table)
    inbound[...] = jnp.zeros_like(inbound)

    def forward_step(b, carry):
        _, joined, z, hidden, n, rstd, edges_next = edges_forward(
            b, count, table, nodes_ref, edges_ref, srow_ref, rrow_ref, w1_ref, w2_ref, g1_ref,
            inbound
        )
        edges_out[block_of(b), :] = edges_next
        joined_all[block_of(b), :] = joined
        z_all[block_of(b), :] = z
        hidden_all[block_of(b), :] = hidden
        n_all[block_of(b), :] = n
        rstd_all[block_of(b), :] = jnp.broadcast_to(rstd, (BLOCK, L))
        return carry

    lax.fori_loop(0, BLOCKS, forward_step, 0)
    nodes_b = nodes_ref[...]
    joined, z, hidden, n, rstd, nodes_next = nodes_forward(
        nodes_b, inbound[...].astype(BF16), u1_ref, u2_ref, g2_ref
    )
    nodes_out[...] = nodes_next
    node_grad = node_grad_ref[...].astype(F32)
    sums[...] = jnp.zeros_like(sums)
    through, dinbound[...] = nodes_backward(
        node_grad, joined, z, hidden, n, rstd, u1_ref, u2_ref, g2_ref, sums
    )
    node_grad_out[...] = node_grad + through
    dtable[...] = jnp.zeros_like(dtable)

    def backward_step(b, carry):
        at = block_of(b)
        edge_grad = edges_backward(
            b, count, joined_all[at, :], z_all[at, :], hidden_all[at, :], n_all[at, :],
            rstd_all[at, :], edge_grad_ref, dinbound, srow_ref, rrow_ref, w1_ref, w2_ref, g1_ref,
            sums, node_grad_out, dtable
        )
        edge_grad_out[at, :] = edge_grad.astype(BF16)
        return carry

    lax.fori_loop(0, BLOCKS, backward_step, 0)
    pack(sums, packed_out)
    ghost_grads(dtable, ghost_grad_out)
    node_grad_out[...] += dtable[0:NODES, 0:L]


def last_kernel(
    count_ref, nodes_ref, inbound_ref, sent_ref, edges_ref, srow_ref, rrow_ref, ghost_row_ref,
    w1_ref, w2_ref, g1_ref, u1_ref, u2_ref, g2_ref, partial_ref, returned_ref, edge_grad_ref,
    ghost_grad_out, edge_grad_out, node_grad_out, packed_out, dinbound, dtable, sums
):
    count = count_ref[0, 0]
    node_grad = add_returned(partial_ref[...], returned_ref, ghost_row_ref)
    node_grad = node_grad.astype(BF16).astype(F32)
    joined, z, hidden, n, rstd, _ = nodes_forward(
        nodes_ref[...], inbound_ref[...], u1_ref, u2_ref, g2_ref
    )
    sums[...] = jnp.zeros_like(sums)
    through, dinbound[...] = nodes_backward(
        node_grad, joined, z, hidden, n, rstd, u1_ref, u2_ref, g2_ref, sums
    )
    node_grad_out[...] = node_grad + through
    dtable[...] = jnp.zeros_like(dtable)

    def backward_step(b, carry):
        at = block_of(b)
        received = dot(receive_hits(b, rrow_ref), nodes_ref[tile_of(b), :]).astype(BF16)
        joined, z = edge_hidden(sent_ref[at, :], received, edges_ref[at, :], w1_ref)
        hidden = (z * sigmoid(z)).astype(BF16)
        n, rstd = layer_norm(dot(hidden, w2_ref[...]))
        edge_grad_out[at, :] = edges_backward(
            b, count, joined, z, hidden, n, rstd, edge_grad_ref, dinbound, srow_ref, rrow_ref,
            w1_ref, w2_ref, g1_ref, sums, node_grad_out, dtable
        )
        return carry

    lax.fori_loop(0, BLOCKS, backward_step, 0)
    pack(sums, packed_out)
    ghost_grads(dtable, ghost_grad_out)
    node_grad_out[...] += dtable[0:NODES, 0:L]


def return_kernel(partial_ref, returned_ref, ghost_row_ref, out_ref):
    out_ref[...] = add_returned(partial_ref[...], returned_ref, ghost_row_ref)


def call(kernel, outs, scratch, scalars, *args):
    vmem = pl.BlockSpec(memory_space=pltpu.VMEM)
    smem = pl.BlockSpec(memory_space=pltpu.SMEM)
    return pl.pallas_call(
        kernel,
        out_shape=[jax.ShapeDtypeStruct(s, d) for s, d in outs],
        in_specs=[smem] * scalars + [vmem] * (len(args) - scalars),
        out_specs=[vmem] * len(outs),
        scratch_shapes=[pltpu.VMEM(s, d) for s, d in scratch],
        compiler_params=pltpu.CompilerParams(vmem_limit_bytes=40 * 1024 * 1024),
    )(*args)


def exchange(slabs):
    up = [(i, i + 1) for i in range(lax.axis_size("gx") - 1)]
    down = [(j, i) for i, j in up]
    rows = slabs.reshape(SLOTS, G, L)
    low, high = (rows[0:3], rows[5:8])
    from_before = lax.ppermute(high, "gx", up)
    from_after = lax.ppermute(low, "gx", down)
    left = jnp.stack([from_before[0], rows[3], from_after[0]], axis=0)
    right = jnp.stack([from_before[2], rows[4], from_after[2]], axis=0)
    up = [(i, i + 1) for i in range(lax.axis_size("gy") - 1)]
    down = [(j, i) for i, j in up]
    before = lax.ppermute(right, "gy", up)
    after = lax.ppermute(left, "gy", down)
    return jnp.concatenate(
        [
            before[0], from_before[1], after[0], before[1], after[1], before[2], from_after[1],
            after[2],
        ],
        axis=0,
    )


def sum_over_domains(packed):
    axes = ("gx", "gy")
    devices = lax.axis_size(axes)
    parts = packed.reshape(devices, -1, L)
    parts = lax.all_to_all(parts, axes, 0, 0, tiled=True)
    mine = jnp.sum(parts.astype(F32), axis=0).astype(BF16)
    copies = jnp.broadcast_to(mine[None], parts.shape)
    whole = lax.all_to_all(copies, axes, 0, 0, tiled=True)
    return whole.reshape(LAYERS, PACKED, L).astype(F32)


def on_device(
    latents,
    edge_latents,
    senders,
    receivers,
    ghost_rows,
    edge_count,
    node_cotangent,
    edge_cotangent,
    edge_first,
    edge_second,
    edge_scale,
    node_first,
    node_second,
    node_scale,
):
    nodes0 = latents[0, 0]
    edges0 = edge_latents[0, 0]
    ids = senders[0, 0]
    srow = jnp.where(ids >= NODES + 4 * G, ids - G, ids).astype(F32).reshape(-1, 128)
    rrow = receivers[0, 0].astype(F32).reshape(-1, 128)
    slots = ghost_rows[0, 0].reshape(9, G)
    grow = jnp.concatenate([slots[:4], slots[5:]], axis=0).astype(F32)

    def weights(i):
        return (
            edge_first[i],
            edge_second[i],
            edge_scale[i : i + 1],
            node_first[i],
            node_second[i],
            node_scale[i : i + 1],
        )

    node_b = ((NODES, L), BF16)
    node_f = ((NODES, L), F32)
    edge_b = ((EDGES, L), BF16)
    edge_f = ((EDGES, L), F32)
    ghost_b = ((GHOSTS, L), BF16)
    packed = ((PACKED, L), BF16)
    packed_f = ((PACKED, L), F32)
    table_b = ((HALF, 2 * L), BF16)
    table_f = ((HALF, 2 * L), F32)

    (picked,) = call(pick_kernel, [ghost_b], [], 0, nodes0, grow)
    ghosts = exchange(picked)
    nodes1, edges1, sent, inbound, picked = call(
        first_kernel, [node_b, edge_b, edge_b, node_b, ghost_b], [table_b, node_f], 1,
        edge_count, nodes0, ghosts, edges0, srow, rrow, grow, *weights(0)
    )
    ghosts = exchange(picked)
    nodes2, edges2, ghost_grad, edge_grad, partial, packed1 = call(
        middle_kernel, [node_b, edge_b, ghost_b, edge_b, node_f, packed],
        [table_b, node_f, ((EDGES, 3 * L), BF16), edge_f, edge_b, edge_f, edge_f, node_b, table_f,
         packed_f],
        1, edge_count, nodes1, ghosts, edges1, srow, rrow, *weights(1), node_cotangent[0, 0],
        edge_cotangent[0, 0]
    )
    returned = exchange(ghost_grad)
    ghost_grad, edge_grad, partial, packed0 = call(
        last_kernel, [ghost_b, edge_f, node_f, packed], [node_b, table_f, packed_f], 1,
        edge_count, nodes0, inbound, sent, edges0, srow, rrow, grow, *weights(0), partial,
        returned, edge_grad
    )
    returned = exchange(ghost_grad)
    (node_grad,) = call(return_kernel, [node_f], [], 0, partial, returned, grow)
    total = sum_over_domains(jnp.concatenate([packed0, packed1], axis=0))
    return (
        nodes2[None, None],
        edges2[None, None],
        node_grad[None, None],
        edge_grad[None, None],
        total[:, 0:384],
        total[:, 384:512],
        total[:, 896] + total[:, 898],
        total[:, 512:768],
        total[:, 768:896],
        total[:, 897] + total[:, 899],
    )


def solution(mesh):
    domain = P("gx", "gy", None, None)
    placed = (
        domain,
        domain,
        P("gx", "gy", None),
        P("gx", "gy", None),
        P("gx", "gy", None, None, None),
        P("gx", "gy"),
        domain,
        domain,
        P(),
        P(),
        P(),
        P(),
        P(),
        P(),
    )
    return jax.shard_map(
        on_device,
        mesh=mesh,
        in_specs=placed,
        out_specs=(domain, domain, domain, domain, P(), P(), P(), P(), P(), P()),
        check_vma=False,
    )
```

```python
import functools

import jax
import jax.numpy as jnp
from jax import lax
from jax.experimental import pallas as pl
from jax.experimental.pallas import tpu as pltpu
from jax.sharding import PartitionSpec as P

L = 128
LAYERS = 2
TILE = 256
DEG = 8
G = 128
NODES = 512
EDGES = 4096
PART = TILE * DEG
BLOCK = 1024
BLOCKS = EDGES // BLOCK
PART_BLOCKS = PART // BLOCK
PACKED = 1024
OUTER = ((0, 0), (0, 1), (0, 2), (1, 0), (1, 2), (2, 0), (2, 1), (2, 2))

F32 = jnp.float32
BF16 = jnp.bfloat16
epsilon = 1e-05


def dot(a, b):
    return jnp.dot(a, b, preferred_element_type=F32)


def dot_nt(a, b):
    return lax.dot_general(a, b, (((1,), (1,)), ((), ())), preferred_element_type=F32)


def dot_tn(a, b):
    return lax.dot_general(a, b, (((0,), (0,)), ((), ())), preferred_element_type=F32)


def sigmoid(v):
    return 0.5 * jnp.tanh(0.5 * v) + 0.5


def column(row):
    parts = [
        jnp.transpose(jnp.broadcast_to(row[:, i : i + 128], (128, 128)))
        for i in range(0, row.shape[1], 128)
    ]
    return jnp.concatenate(parts, axis=0) if len(parts) > 1 else parts[0]


def hits(col, width):
    lane = lax.broadcasted_iota(jnp.int32, col.shape, 1)
    parts = [
        jnp.where(col == lane + 128 * t, 1.0, 0.0).astype(BF16) for t in range(width // 128)
    ]
    return jnp.concatenate(parts, axis=1)


def hits_t(row, height):
    sub = lax.broadcasted_iota(jnp.int32, (height, row.shape[1]), 0)
    return jnp.where(sub == row, 1.0, 0.0).astype(BF16)


def layer_norm(y):
    center = y - jnp.mean(y, axis=-1, keepdims=True)
    spread = jnp.mean(center * center, axis=-1, keepdims=True)
    rstd = lax.rsqrt(spread + epsilon)
    return center * rstd, rstd


def layer_norm_grad(dn, n, rstd):
    return rstd * (
        dn
        - jnp.mean(dn, axis=-1, keepdims=True)
        - n * jnp.mean(dn * n, axis=-1, keepdims=True)
    )


def silu_grad(z):
    s = sigmoid(z)
    return s * (1.0 + z * (1.0 - s))


def block_at(b):
    return pl.ds(pl.multiple_of(b * BLOCK, BLOCK), BLOCK)


def tile_at(b):
    return pl.ds(pl.multiple_of((b // PART_BLOCKS) * TILE, TILE), TILE)


def index_row(ref, b):
    return ref[:, block_at(b)]


def local_index(ids):
    return jnp.where(ids < TILE, ids, jnp.where(ids < NODES, ids - TILE, -1))


def ghost_index(ids):
    g = ids - NODES
    g = jnp.where(g >= 4 * G, g - G, g)
    return jnp.where(g >= NODES, g - NODES, g)


def ghost_upper(ids):
    return ids >= NODES + NODES + G


def live_of(b, count):
    slot = lax.broadcasted_iota(jnp.int32, (BLOCK, L), 0) + b * BLOCK
    return jnp.where(slot < count, 1.0, 0.0)


def pick(nodes_b, ghost_row_ref, slabs):
    for s, (i, j) in enumerate(OUTER):
        col = column(ghost_row_ref[i, j : j + 1, :])
        put_slab(slabs, s, dot(hits(col, NODES), nodes_b).astype(BF16))


def put_slab(slabs, s, value):
    low, same, high = slabs
    ref, i = ((low, s), (same, s - 3), (high, s - 5))[(s >= 3) + (s >= 5)]
    ref[i] = value


def arrived(refs):
    before, from_before, after, from_after = refs
    return [
        before[0], from_before[1], after[0], before[1], after[1], before[2], from_after[1], after[2]
    ]


def local_pair(nodes_ref):
    return jnp.concatenate([nodes_ref[0:TILE, :], nodes_ref[TILE:NODES, :]], axis=1)


def ghost_pair(ghost_refs):
    rows = arrived(ghost_refs)
    lower = jnp.concatenate(rows[:4], axis=0)
    upper = jnp.concatenate(rows[4:], axis=0)
    return jnp.concatenate([lower, upper], axis=1)


def nodes_forward(nodes_b, inbound_b, u1, u2, gain):
    joined = jnp.concatenate([nodes_b, inbound_b], axis=1)
    z = dot(joined, u1)
    hidden = (z * sigmoid(z)).astype(BF16)
    n, rstd = layer_norm(dot(hidden, u2))
    nodes_next = (nodes_b.astype(F32) + n * gain).astype(BF16)
    return joined, z, hidden, n, rstd, nodes_next


def nodes_backward(grad, joined, z, hidden, n, rstd, u1, u2, gain, sums):
    sums[384:512, :] = dot_tn(hidden, (dy := layer_norm_grad(grad * gain, n, rstd).astype(BF16)))
    sums[513:514, :] = jnp.sum(grad * n, axis=0, keepdims=True)
    dz = (dot_nt(dy, u2).astype(BF16).astype(F32) * silu_grad(z)).astype(BF16)
    sums[128:384, :] = dot_tn(joined, dz)
    back = dot_nt(dz, u1).astype(BF16)
    return back[:, :L].astype(F32), back[:, L:]


def before_kernel(part, layer, nodes_ref, edges_ref, send_ref, recv_ref, w1_ref, sent_out,
                  received_out, z_out):
    pair = local_pair(nodes_ref)
    tile = nodes_ref[part * TILE : (part + 1) * TILE, :]
    w1 = w1_ref[layer]

    def step(i, carry):
        b = i + part * PART_BLOCKS
        ids = index_row(send_ref, b)
        both = dot(hits(column(local_index(ids)), TILE), pair)
        sent = jnp.where(column(ids) >= TILE, both[:, L:], both[:, :L]).astype(BF16)
        received = dot(hits(column(index_row(recv_ref, b)), TILE), tile).astype(BF16)
        sent_out[block_at(i), :] = sent
        received_out[block_at(i), :] = received
        joined = jnp.concatenate([sent, received, edges_ref[block_at(b), :]], axis=1)
        z_out[block_at(i), :] = dot(joined, w1)
        return carry

    lax.fori_loop(0, PART_BLOCKS, step, 0, unroll=True)


def edges_forward(b, local, count, table, edges_ref, send_ref, recv_ref, w1s, w2, gain, inbound,
                  edges_out, sent_out, z_out, n_out, rstd_out):
    sent_ref, z_ref, i = local
    ids = index_row(send_ref, b)
    both = dot(hits(column(ghost_index(ids)), NODES), table)
    sent = jnp.where(column(ids) >= 2 * NODES + G, both[:, L:], both[:, :L]).astype(BF16)
    z = z_ref[block_at(i), :] + dot(sent, w1s)
    hidden = (z * sigmoid(z)).astype(BF16)
    n, rstd = layer_norm(dot(hidden, w2))
    message = n * gain * live_of(b, count)
    at = block_at(b)
    edges_out[at, :] = (edges_ref[at, :].astype(F32) + message).astype(BF16)
    inbound[tile_at(b), :] += dot(hits_t(index_row(recv_ref, b), TILE), message.astype(BF16))
    sent_out[at, :] = sent_ref[block_at(i), :] + sent
    z_out[at, :] = z
    n_out[at, :] = n
    rstd_out[at, :] = jnp.broadcast_to(rstd, (BLOCK, L))


def all_edges_forward(count, locals_, ghost_refs, table, edges_ref, send_ref, recv_ref, w1s, w2,
                      gain, inbound, outs):
    table[...] = ghost_pair(ghost_refs)
    inbound[...] = jnp.zeros_like(inbound)
    for part in range(2):
        sent_ref, z_ref = locals_[2 * part : 2 * part + 2]

        def step(i, carry, part=part, sent_ref=sent_ref, z_ref=z_ref):
            edges_forward(
                i + part * PART_BLOCKS, (sent_ref, z_ref, i), count, table[...], edges_ref,
                send_ref, recv_ref, w1s, w2, gain, inbound, *outs
            )
            return carry

        lax.fori_loop(0, PART_BLOCKS, step, 0, unroll=True)


def edges_backward(b, count, grad_ref, dinbound, z_ref, n_ref, rstd_ref, send_ref, recv_ref, w1s,
                   w2, gain, dy_out, dz_out, dsent_out, gain_sum, dtable):
    at = block_at(b)
    n = n_ref[at, :]
    from_nodes = dot(hits(column(index_row(recv_ref, b)), TILE), dinbound[tile_at(b), :])
    dmessage = (grad_ref[at, :].astype(F32) + from_nodes) * live_of(b, count)
    gain_sum[0:1, :] += jnp.sum(dmessage * n, axis=0, keepdims=True)
    dy = layer_norm_grad(dmessage * gain, n, rstd_ref[at, :]).astype(BF16)
    dz = (dot_nt(dy, w2).astype(BF16).astype(F32) * silu_grad(z_ref[at, :])).astype(BF16)
    dsent = dot_nt(dz, w1s).astype(BF16)
    dy_out[at, :] = dy
    dz_out[at, :] = dz
    dsent_out[at, :] = dsent
    ids = index_row(send_ref, b)
    upper = column(ids) >= 2 * NODES + G
    dsent32 = dsent.astype(F32)
    pair = jnp.concatenate(
        [jnp.where(upper, 0.0, dsent32).astype(BF16), jnp.where(upper, dsent32, 0.0).astype(BF16)],
        axis=1,
    )
    dtable[...] += dot(hits_t(ghost_index(ids), NODES), pair)


def all_edges_backward(count, grad_ref, dinbound, residuals, send_ref, recv_ref, w1s, w2, gain,
                       outs, gain_sum, dtable, ghost_grad_out):
    gain_sum[...] = jnp.zeros_like(gain_sum)
    dtable[...] = jnp.zeros_like(dtable)

    def step(b, carry):
        edges_backward(
            b, count, grad_ref, dinbound, *residuals, send_ref, recv_ref, w1s, w2, gain, *outs,
            gain_sum, dtable
        )
        return carry

    lax.fori_loop(0, BLOCKS, step, 0, unroll=True)
    for s in range(8):
        rows, half = pl.ds((s % 4) * G, G), pl.ds((s // 4) * L, L)
        put_slab(ghost_grad_out, s, dtable[rows, half].astype(BF16))


def after_kernel(part, layer, sent_ref, received_ref, edges_ref, z_ref, dy_ref, dz_ref, dsent_ref,
                 send_ref, recv_ref, w1_ref, edge_grad_ref, *rest):
    if part:
        dw1_in, dw2_in, dlocal_in, dtile_in, sums_ref, partial_ref = rest[:6]
        edge_grad_out, partial_out, packed_out, dw1, dw2, dlocal, dtile = rest[6:]
        dw1[...] = dw1_in[...]
        dw2[...] = dw2_in[...]
        dlocal[...] = dlocal_in[...]
    else:
        edge_grad_out, dw1, dw2, dlocal, dtile = rest
        dw1[...] = jnp.zeros_like(dw1)
        dw2[...] = jnp.zeros_like(dw2)
        dlocal[...] = jnp.zeros_like(dlocal)
    dtile[...] = jnp.zeros_like(dtile)
    w1re = w1_ref[layer, L:, :]

    def step(i, carry):
        b = i + part * PART_BLOCKS
        at = block_at(b)
        z = z_ref[at, :]
        dz = dz_ref[at, :]
        dw2[...] += dot_tn((z * sigmoid(z)).astype(BF16), dy_ref[at, :])
        joined = jnp.concatenate(
            [sent_ref[at, :], received_ref[block_at(i), :], edges_ref[at, :]], axis=1
        )
        dw1[...] += dot_tn(joined, dz)
        back = dot_nt(dz, w1re).astype(BF16)
        grad_at = at if edge_grad_ref.shape[0] == EDGES else block_at(i)
        edge_grad = edge_grad_ref[grad_at, :].astype(F32) + back[:, L:].astype(F32)
        edge_grad_out[block_at(i), :] = edge_grad.astype(edge_grad_out.dtype)
        dtile[...] += dot(hits_t(index_row(recv_ref, b), TILE), back[:, :L])
        ids = index_row(send_ref, b)
        upper = column(ids) >= TILE
        dsent32 = dsent_ref[at, :].astype(F32)
        pair = jnp.concatenate(
            [
                jnp.where(upper, 0.0, dsent32).astype(BF16),
                jnp.where(upper, dsent32, 0.0).astype(BF16),
            ],
            axis=1,
        )
        dlocal[...] += dot(hits_t(local_index(ids), TILE), pair)
        return carry

    lax.fori_loop(0, PART_BLOCKS, step, 0, unroll=True)
    if part:
        partial_out[0:TILE, :] = partial_ref[0:TILE, :] + dtile_in[...] + dlocal[:, :L]
        partial_out[TILE:, :] = partial_ref[TILE:, :] + dtile[...] + dlocal[:, L:]
        gains = sums_ref[512:520, :]
        high = gains.astype(BF16).astype(F32)
        packed_out[0:384, :] = dw1[...].astype(BF16)
        packed_out[384:512, :] = dw2[...].astype(BF16)
        packed_out[512:896, :] = sums_ref[128:512, :].astype(BF16)
        packed_out[896:912, :] = jnp.concatenate([high, gains - high], axis=0).astype(BF16)
        packed_out[912:PACKED, :] = jnp.zeros((PACKED - 912, L), BF16)


def pick_kernel(nodes_ref, ghost_row_ref, *slabs):
    pick(nodes_ref[...], ghost_row_ref, slabs)


def turn_kernel(from_before, same, from_after, left, right):
    left[0] = from_before[0]
    left[1] = same[0]
    left[2] = from_after[0]
    right[0] = from_before[2]
    right[1] = same[1]
    right[2] = from_after[2]


def first_kernel(
    count_ref, nodes_ref, edges_ref, send_ref, recv_ref, ghost_row_ref, w1_ref, w2_ref, g1_ref,
    u1_ref, u2_ref, g2_ref, sent0, z0, sent1, z1, *rest
):
    ghost_refs, rest = rest[:4], rest[4:]
    nodes_out, inbound_out, *slabs = rest[:5]
    outs, (table, inbound) = rest[5:10], rest[10:]
    all_edges_forward(
        count_ref[0, 0], (sent0, z0, sent1, z1), ghost_refs, table, edges_ref, send_ref, recv_ref,
        w1_ref[0, :L, :], w2_ref[0], g1_ref[0:1, :], inbound, outs
    )
    inbound_b = inbound[...].astype(BF16)
    inbound_out[...] = inbound_b
    nodes_next = nodes_forward(nodes_ref[...], inbound_b, u1_ref[0], u2_ref[0], g2_ref[0:1, :])[-1]
    nodes_out[...] = nodes_next
    pick(nodes_next, ghost_row_ref, slabs)


def start_nodes_backward(grad, nodes_b, inbound_b, layer, u1_ref, u2_ref, g2_ref, sums):
    u1, u2, gain = u1_ref[layer], u2_ref[layer], g2_ref[layer : layer + 1, :]
    sums[512:520, :] = jnp.zeros((8, L), F32)
    *saved, nodes_next = nodes_forward(nodes_b, inbound_b, u1, u2, gain)
    through, dinbound = nodes_backward(grad, *saved, u1, u2, gain, sums)
    return nodes_next, grad + through, dinbound


def middle_kernel(
    count_ref, nodes_ref, edges_ref, send_ref, recv_ref, w1_ref, w2_ref, g1_ref, u1_ref, u2_ref,
    g2_ref, node_grad_ref, edge_grad_ref, sent0, z0, sent1, z1, *rest
):
    ghost_refs, rest = rest[:4], rest[4:]
    nodes_out, edges_out, sent_out, z_out, dy_out, dz_out, dsent_out = rest[:7]
    partial_out, sums, *ghost_grad_out = rest[7:12]
    table, inbound, n_all, rstd_all, dinbound, dtable, gain_sum = rest[12:]
    count = count_ref[0, 0]
    w1s, w2, gain = w1_ref[1, :L, :], w2_ref[1], g1_ref[1:2, :]
    all_edges_forward(
        count, (sent0, z0, sent1, z1), ghost_refs, table, edges_ref, send_ref, recv_ref, w1s, w2,
        gain, inbound, (edges_out, sent_out, z_out, n_all, rstd_all)
    )
    nodes_out[...], partial_out[...], dinbound[...] = start_nodes_backward(
        node_grad_ref[...].astype(F32), nodes_ref[...], inbound[...].astype(BF16), 1, u1_ref,
        u2_ref, g2_ref, sums
    )
    all_edges_backward(
        count, edge_grad_ref, dinbound, (z_out, n_all, rstd_all), send_ref, recv_ref, w1s, w2, gain,
        (dy_out, dz_out, dsent_out), gain_sum, dtable, ghost_grad_out
    )
    sums[512:513, :] = gain_sum[0:1, :]


def last_kernel(
    count_ref, nodes_ref, inbound_ref, send_ref, recv_ref, ghost_row_ref, w1_ref, w2_ref, g1_ref,
    u1_ref, u2_ref, g2_ref, partial_ref, edge_grad0_ref, edge_grad1_ref, z_ref, n_ref, rstd_ref,
    *rest
):
    returned_refs, rest = rest[:4], rest[4:]
    dy_out, dz_out, dsent_out, partial_out, sums, *ghost_grad_out = rest[:8]
    dinbound, dtable, gain_sum, edge_grad = rest[8:]
    node_grad = add_returned(partial_ref[...], returned_refs, ghost_row_ref)
    _, partial_out[...], dinbound[...] = start_nodes_backward(
        node_grad.astype(BF16).astype(F32), nodes_ref[...], inbound_ref[...], 0, u1_ref, u2_ref,
        g2_ref, sums
    )
    edge_grad[0:PART, :] = edge_grad0_ref[...]
    edge_grad[PART:, :] = edge_grad1_ref[...]
    all_edges_backward(
        count_ref[0, 0], edge_grad, dinbound, (z_ref, n_ref, rstd_ref), send_ref, recv_ref,
        w1_ref[0, :L, :], w2_ref[0], g1_ref[0:1, :], (dy_out, dz_out, dsent_out), gain_sum, dtable,
        ghost_grad_out
    )
    sums[512:513, :] = gain_sum[0:1, :]


def add_returned(partial, returned_refs, ghost_row_ref):
    row = jnp.concatenate([ghost_row_ref[i, j : j + 1, :] for i, j in OUTER], axis=1)
    returned = jnp.concatenate(arrived(returned_refs), axis=0)
    return partial + dot(hits_t(row, NODES), returned)


def return_kernel(partial_ref, ghost_row_ref, *rest):
    rest[4][...] = add_returned(partial_ref[...], rest[:4], ghost_row_ref)


def call(kernel, name, outs, scratch, scalars, flops, *args):
    vmem = pl.BlockSpec(memory_space=pltpu.VMEM)
    smem = pl.BlockSpec(memory_space=pltpu.SMEM)
    return pl.pallas_call(
        kernel,
        name=name,
        out_shape=[jax.ShapeDtypeStruct(s, d) for s, d in outs],
        in_specs=[smem] * scalars + [vmem] * (len(args) - scalars),
        out_specs=[vmem] * len(outs),
        scratch_shapes=[pltpu.VMEM(s, d) for s, d in scratch],
        cost_estimate=pl.CostEstimate(flops=flops, bytes_accessed=1 << 20, transcendentals=0),
        compiler_params=pltpu.CompilerParams(vmem_limit_bytes=24 * 1024 * 1024),
    )(*args)


def shifts(axis):
    up = [(i, i + 1) for i in range(lax.axis_size(axis) - 1)]
    return up, [(j, i) for i, j in up]


def exchange(slabs, beside):
    low, same, high = slabs
    up, down = shifts("gx")
    from_before = lax.ppermute(high, "gx", up)
    from_after = lax.ppermute(low, "gx", down)
    first = beside(0, None)
    left, right = call(
        turn_kernel, "turn", [(low.shape, BF16)] * 2, [], 0, 10**6, from_before, same, from_after
    )
    up, down = shifts("gy")
    before = lax.ppermute(right, "gy", up)
    after = lax.ppermute(left, "gy", down)
    second = beside(1, (first, right))
    return (before, from_before, after, from_after), first, second


def sum_over_domains(packed):
    axes = ("gx", "gy")
    sizes = (lax.axis_size("gx"), lax.axis_size("gy"))
    plane, line = planes_and_lines(*sizes)

    def trade(parts, groups):
        return lax.all_to_all(parts, axes, 0, 0, tiled=True, axis_index_groups=groups)

    def copies(part, groups):
        return trade(jnp.broadcast_to(part[None], (len(groups[0]),) + part.shape), groups)

    parts = trade(packed.reshape(len(plane[0]), -1, L), plane)
    mine = jnp.sum(parts.astype(F32), axis=0).astype(BF16)
    mine = jnp.sum(copies(mine, line).astype(F32), axis=0).astype(BF16)
    return copies(mine, plane).reshape(LAYERS, PACKED, L)


def planes_and_lines(rows, columns):
    planes, lines = {}, {}
    for i in range(rows * columns):
        gx, gy = divmod(i, columns)
        y, z_low = divmod(gx, 4)
        z_high, rest = divmod(gy, 8)
        planes.setdefault((z_high, z_low), []).append(i)
        lines.setdefault((y, rest), []).append(i)
    return list(planes.values()), list(lines.values())


def unpack_kernel(total_ref, dw1, dw2, dg1, du1, du2, dg2):
    for i in range(LAYERS):
        dw1[i] = total_ref[i, 0:384, :].astype(F32)
        dw2[i] = total_ref[i, 384:512, :].astype(F32)
        du1[i] = total_ref[i, 512:768, :].astype(F32)
        du2[i] = total_ref[i, 768:896, :].astype(F32)
        gains = total_ref[i, 896:912, :].astype(F32)
        dg1[i : i + 1, :] = gains[0:1, :] + gains[8:9, :]
        dg2[i : i + 1, :] = gains[1:2, :] + gains[9:10, :]


def on_device(
    latents,
    edge_latents,
    senders,
    receivers,
    ghost_rows,
    edge_count,
    node_cotangent,
    edge_cotangent,
    edge_first,
    edge_second,
    edge_scale,
    node_first,
    node_second,
    node_scale,
):
    nodes0 = latents[0, 0]
    edges0 = edge_latents[0, 0]
    ids = senders[0]
    targets = receivers[0]
    grow = ghost_rows[0, 0]
    weights = (edge_first, edge_second, edge_scale, node_first, node_second, node_scale)

    node_b = ((NODES, L), BF16)
    node_f = ((NODES, L), F32)
    edge_b = ((EDGES, L), BF16)
    edge_f = ((EDGES, L), F32)
    part_b = ((PART, L), BF16)
    part_f = ((PART, L), F32)
    slabs_b = [((n, G, L), BF16) for n in (3, 2, 3)]
    packed_b = ((PACKED, L), BF16)
    sums_f = ((520, L), F32)
    pair_b = ((NODES, 2 * L), BF16)
    pair_f = ((NODES, 2 * L), F32)
    gain_f = ((8, L), F32)
    dw1_f = ((3 * L, L), F32)
    dw2_f = ((L, L), F32)
    dlocal_f = ((TILE, 2 * L), F32)
    dtile_f = ((TILE, L), F32)

    def before(layer, nodes, edges):
        def part_of(part, wait):
            node_arg = nodes
            if wait is not None:
                node_arg, _ = lax.optimization_barrier((nodes, wait))
            return call(
                functools.partial(before_kernel, part, layer), f"before{layer}{part}",
                [part_b, part_b, part_f], [], 0, 2 * 10**9, node_arg, edges, ids, targets,
                edge_first
            )

        return part_of

    def after(layer, sent, received, edges, z, dy, dz, dsent, edge_grads, out, sums, partial):
        def part_of(part, wait):
            dy_arg, extra = dy, ()
            if part:
                dy_arg, _ = lax.optimization_barrier((dy, wait[1]))
                extra = (*wait[0][1:], sums, partial)
            outs = [(part_b[0], out)]
            outs += [node_f, packed_b] if part else [dw1_f, dw2_f, dlocal_f, dtile_f]
            return call(
                functools.partial(after_kernel, part, layer), f"after{layer}{part}", outs,
                [dw1_f, dw2_f, dlocal_f, dtile_f] if part else [], 0, 2 * 10**9, sent,
                received[part], edges, z, dy_arg, dz, dsent, ids, targets, edge_first, edge_grads[part],
                *extra
            )

        return part_of

    picked = call(pick_kernel, "pick", slabs_b, [], 0, 10**8, nodes0, grow)
    ghosts, a0, a1 = exchange(picked, before(0, nodes0, edges0))
    nodes1, inbound, *picked, edges1, sent_0, z_0, n_0, rstd_0 = call(
        first_kernel, "first", [node_b, node_b, *slabs_b, edge_b, edge_b, edge_f, edge_f, edge_f],
        [pair_b, node_f], 1, 4 * 10**9, edge_count, nodes0, edges0, ids, targets, grow, *weights,
        a0[0], a0[2], a1[0], a1[2], *ghosts
    )
    received_0 = (a0[1], a1[1])
    ghosts, a0, a1 = exchange(picked, before(1, nodes1, edges1))
    received_1 = (a0[1], a1[1])
    nodes2, edges2, sent_1, z_1, dy, dz, dsent, partial, sums, *ghost_grad = call(
        middle_kernel, "middle",
        [node_b, edge_b, edge_b, edge_f, edge_b, edge_b, edge_b, node_f, sums_f, *slabs_b],
        [pair_b, node_f, edge_f, edge_f, node_b, pair_f, gain_f], 1, 8 * 10**9, edge_count, nodes1,
        edges1, ids, targets, *weights, node_cotangent[0, 0], edge_cotangent[0, 0], a0[0], a0[2],
        a1[0], a1[2], *ghosts
    )
    returned, c0, c1 = exchange(
        ghost_grad,
        after(1, sent_1, received_1, edges1, z_1, dy, dz, dsent, (edge_cotangent[0, 0],) * 2, BF16,
              sums, partial),
    )
    edge_grad0, (edge_grad1, partial, packed1) = c0[0], c1
    dy, dz, dsent, partial, sums, *ghost_grad = call(
        last_kernel, "last", [edge_b, edge_b, edge_b, node_f, sums_f, *slabs_b],
        [node_b, pair_f, gain_f, edge_b], 1, 4 * 10**9, edge_count, nodes0, inbound, ids, targets,
        grow, *weights, partial, edge_grad0, edge_grad1, z_0, n_0, rstd_0, *returned
    )
    returned, c0, c1 = exchange(
        ghost_grad,
        after(0, sent_0, received_0, edges0, z_0, dy, dz, dsent, (edge_grad0, edge_grad1), F32, sums,
              partial),
    )
    edge_grad0, (edge_grad1, partial, packed0) = c0[0], c1
    (node_grad,) = call(
        return_kernel, "returned", [node_f], [], 0, 10**8, partial, grow, *returned
    )
    total = sum_over_domains(jnp.concatenate([packed0, packed1], axis=0))
    grads = call(
        unpack_kernel, "unpack", [((LAYERS,) + w.shape[1:], F32) for w in weights], [], 0, 10**6,
        total
    )
    return (
        nodes2[None, None],
        edges2[None, None],
        node_grad[None, None],
        jnp.concatenate([edge_grad0, edge_grad1], axis=0)[None, None],
        *grads,
    )


def solution(mesh):
    domain = P("gx", "gy", None, None)
    placed = (
        domain,
        domain,
        P("gx", "gy", None),
        P("gx", "gy", None),
        P("gx", "gy", None, None, None),
        P("gx", "gy"),
        domain,
        domain,
        P(),
        P(),
        P(),
        P(),
        P(),
        P(),
    )
    return jax.shard_map(
        on_device,
        mesh=mesh,
        in_specs=placed,
        out_specs=(domain, domain, domain, domain, P(), P(), P(), P(), P(), P()),
        check_vma=False,
    )
```

```python
import functools

import jax
import jax.numpy as jnp
from jax import lax
from jax.experimental import pallas as pl
from jax.experimental.pallas import tpu as pltpu
from jax.sharding import PartitionSpec as P

L = 128
LAYERS = 2
TILE = 256
DEG = 8
G = 128
NODES = 512
EDGES = 4096
PART = TILE * DEG
BLOCK = 1024
BLOCKS = EDGES // BLOCK
PART_BLOCKS = PART // BLOCK
PACKED = 1024
OUTER = ((0, 0), (0, 1), (0, 2), (1, 0), (1, 2), (2, 0), (2, 1), (2, 2))

F32 = jnp.float32
BF16 = jnp.bfloat16
epsilon = 1e-05


def dot(a, b):
    return jnp.dot(a, b, preferred_element_type=F32)


def dot_nt(a, b):
    return lax.dot_general(a, b, (((1,), (1,)), ((), ())), preferred_element_type=F32)


def dot_tn(a, b):
    return lax.dot_general(a, b, (((0,), (0,)), ((), ())), preferred_element_type=F32)


def sigmoid(v):
    return 0.5 * jnp.tanh(0.5 * v) + 0.5


def column(row):
    parts = [
        jnp.transpose(jnp.broadcast_to(row[:, i : i + 128], (128, 128)))
        for i in range(0, row.shape[1], 128)
    ]
    return jnp.concatenate(parts, axis=0) if len(parts) > 1 else parts[0]


def hits(col, width):
    lane = lax.broadcasted_iota(jnp.int32, col.shape, 1)
    parts = [
        jnp.where(col == lane + 128 * t, 1.0, 0.0).astype(BF16) for t in range(width // 128)
    ]
    return jnp.concatenate(parts, axis=1)


def hits_t(row, height):
    sub = lax.broadcasted_iota(jnp.int32, (height, row.shape[1]), 0)
    return jnp.where(sub == row, 1.0, 0.0).astype(BF16)


def layer_norm(y):
    center = y - jnp.mean(y, axis=-1, keepdims=True)
    spread = jnp.mean(center * center, axis=-1, keepdims=True)
    rstd = lax.rsqrt(spread + epsilon)
    return center * rstd, rstd


def layer_norm_grad(dn, n, rstd):
    return rstd * (
        dn
        - jnp.mean(dn, axis=-1, keepdims=True)
        - n * jnp.mean(dn * n, axis=-1, keepdims=True)
    )


def silu_grad(z):
    s = sigmoid(z)
    return s * (1.0 + z * (1.0 - s))


def block_at(b):
    return pl.ds(pl.multiple_of(b * BLOCK, BLOCK), BLOCK)


def tile_at(b):
    return pl.ds(pl.multiple_of((b // PART_BLOCKS) * TILE, TILE), TILE)


def index_row(ref, b):
    return ref[:, block_at(b)]


def local_index(ids):
    return jnp.where(ids < TILE, ids, jnp.where(ids < NODES, ids - TILE, -1))


def ghost_index(ids):
    g = ids - NODES
    g = jnp.where(g >= 4 * G, g - G, g)
    return jnp.where(g >= NODES, g - NODES, g)


def ghost_upper(ids):
    return ids >= NODES + NODES + G


def live_of(b, count):
    slot = lax.broadcasted_iota(jnp.int32, (BLOCK, L), 0) + b * BLOCK
    return jnp.where(slot < count, 1.0, 0.0)


def pick(parity_ref, nodes_b, ghost_row_ref, slabs):
    rows = []
    for i, j in OUTER:
        col = column(ghost_row_ref[i, j : j + 1, :])
        rows.append(dot(hits(col, NODES), nodes_b).astype(BF16))
    put_slabs(parity_ref, rows, slabs)


def put_slabs(parity_ref, rows, slabs):
    to_even, to_odd, same = slabs
    is_even = parity_ref[0, 0] == 0
    for i in range(3):
        to_even[i] = jnp.where(is_even, rows[5 + i], rows[i])
        to_odd[i] = jnp.where(is_even, rows[i], rows[5 + i])
    same[0] = rows[3]
    same[1] = rows[4]


def from_both(is_even, even_ref, odd_ref, i):
    even, odd = even_ref[i], odd_ref[i]
    return jnp.where(is_even, odd, even), jnp.where(is_even, even, odd)


def arrived(parity_ref, refs):
    even_x, odd_x, even_y, odd_y = refs
    row = from_both(parity_ref[0, 0] == 0, even_x, odd_x, 1)
    columns = [from_both(parity_ref[0, 1] == 0, even_y, odd_y, i) for i in range(3)]
    return [
        columns[0][0], row[0], columns[0][1], columns[1][0], columns[1][1], columns[2][0], row[1],
        columns[2][1]
    ]


def local_pair(nodes_ref):
    return jnp.concatenate([nodes_ref[0:TILE, :], nodes_ref[TILE:NODES, :]], axis=1)


def ghost_pair(parity_ref, ghost_refs):
    rows = arrived(parity_ref, ghost_refs)
    lower = jnp.concatenate(rows[:4], axis=0)
    upper = jnp.concatenate(rows[4:], axis=0)
    return jnp.concatenate([lower, upper], axis=1)


def nodes_forward(nodes_b, inbound_b, u1, u2, gain):
    joined = jnp.concatenate([nodes_b, inbound_b], axis=1)
    z = dot(joined, u1)
    hidden = (z * sigmoid(z)).astype(BF16)
    n, rstd = layer_norm(dot(hidden, u2))
    nodes_next = (nodes_b.astype(F32) + n * gain).astype(BF16)
    return joined, z, hidden, n, rstd, nodes_next


def nodes_backward(grad, joined, z, hidden, n, rstd, u1, u2, gain, sums):
    sums[384:512, :] = dot_tn(hidden, (dy := layer_norm_grad(grad * gain, n, rstd).astype(BF16)))
    sums[513:514, :] = jnp.sum(grad * n, axis=0, keepdims=True)
    dz = (dot_nt(dy, u2).astype(BF16).astype(F32) * silu_grad(z)).astype(BF16)
    sums[128:384, :] = dot_tn(joined, dz)
    back = dot_nt(dz, u1).astype(BF16)
    return back[:, :L].astype(F32), back[:, L:]


def before_kernel(part, layer, nodes_ref, edges_ref, send_ref, recv_ref, w1_ref, sent_out,
                  received_out, z_out):
    pair = local_pair(nodes_ref)
    tile = nodes_ref[part * TILE : (part + 1) * TILE, :]
    w1 = w1_ref[layer]

    def step(i, carry):
        b = i + part * PART_BLOCKS
        ids = index_row(send_ref, b)
        both = dot(hits(column(local_index(ids)), TILE), pair)
        sent = jnp.where(column(ids) >= TILE, both[:, L:], both[:, :L]).astype(BF16)
        received = dot(hits(column(index_row(recv_ref, b)), TILE), tile).astype(BF16)
        sent_out[block_at(i), :] = sent
        received_out[block_at(i), :] = received
        joined = jnp.concatenate([sent, received, edges_ref[block_at(b), :]], axis=1)
        z_out[block_at(i), :] = dot(joined, w1)
        return carry

    lax.fori_loop(0, PART_BLOCKS, step, 0, unroll=True)


def edges_forward(b, local, count, table, edges_ref, send_ref, recv_ref, w1s, w2, gain, inbound,
                  edges_out, sent_out, z_out, n_out, rstd_out):
    sent_ref, z_ref, i = local
    ids = index_row(send_ref, b)
    both = dot(hits(column(ghost_index(ids)), NODES), table)
    sent = jnp.where(column(ids) >= 2 * NODES + G, both[:, L:], both[:, :L]).astype(BF16)
    z = z_ref[block_at(i), :] + dot(sent, w1s)
    hidden = (z * sigmoid(z)).astype(BF16)
    n, rstd = layer_norm(dot(hidden, w2))
    message = n * gain * live_of(b, count)
    at = block_at(b)
    edges_out[at, :] = (edges_ref[at, :].astype(F32) + message).astype(BF16)
    inbound[tile_at(b), :] += dot(hits_t(index_row(recv_ref, b), TILE), message.astype(BF16))
    sent_out[at, :] = sent_ref[block_at(i), :] + sent
    z_out[at, :] = z
    n_out[at, :] = n
    rstd_out[at, :] = jnp.broadcast_to(rstd, (BLOCK, L))


def all_edges_forward(parity_ref, count, locals_, ghost_refs, table, edges_ref, send_ref, recv_ref, w1s, w2,
                      gain, inbound, outs):
    table[...] = ghost_pair(parity_ref, ghost_refs)
    inbound[...] = jnp.zeros_like(inbound)
    for part in range(2):
        sent_ref, z_ref = locals_[2 * part : 2 * part + 2]

        def step(i, carry, part=part, sent_ref=sent_ref, z_ref=z_ref):
            edges_forward(
                i + part * PART_BLOCKS, (sent_ref, z_ref, i), count, table[...], edges_ref,
                send_ref, recv_ref, w1s, w2, gain, inbound, *outs
            )
            return carry

        lax.fori_loop(0, PART_BLOCKS, step, 0, unroll=True)


def edges_backward(b, count, grad_ref, dinbound, z_ref, n_ref, rstd_ref, send_ref, recv_ref, w1s,
                   w2, gain, dy_out, dz_out, dsent_out, gain_sum, dtable):
    at = block_at(b)
    n = n_ref[at, :]
    from_nodes = dot(hits(column(index_row(recv_ref, b)), TILE), dinbound[tile_at(b), :])
    dmessage = (grad_ref[at, :].astype(F32) + from_nodes) * live_of(b, count)
    gain_sum[0:1, :] += jnp.sum(dmessage * n, axis=0, keepdims=True)
    dy = layer_norm_grad(dmessage * gain, n, rstd_ref[at, :]).astype(BF16)
    dz = (dot_nt(dy, w2).astype(BF16).astype(F32) * silu_grad(z_ref[at, :])).astype(BF16)
    dsent = dot_nt(dz, w1s).astype(BF16)
    dy_out[at, :] = dy
    dz_out[at, :] = dz
    dsent_out[at, :] = dsent
    ids = index_row(send_ref, b)
    upper = column(ids) >= 2 * NODES + G
    dsent32 = dsent.astype(F32)
    pair = jnp.concatenate(
        [jnp.where(upper, 0.0, dsent32).astype(BF16), jnp.where(upper, dsent32, 0.0).astype(BF16)],
        axis=1,
    )
    dtable[...] += dot(hits_t(ghost_index(ids), NODES), pair)


def all_edges_backward(parity_ref, count, grad_ref, dinbound, residuals, send_ref, recv_ref, w1s, w2, gain,
                       outs, gain_sum, dtable, ghost_grad_out):
    gain_sum[...] = jnp.zeros_like(gain_sum)
    dtable[...] = jnp.zeros_like(dtable)

    def step(b, carry):
        edges_backward(
            b, count, grad_ref, dinbound, *residuals, send_ref, recv_ref, w1s, w2, gain, *outs,
            gain_sum, dtable
        )
        return carry

    lax.fori_loop(0, BLOCKS, step, 0, unroll=True)
    rows = []
    for s in range(8):
        at, half = pl.ds((s % 4) * G, G), pl.ds((s // 4) * L, L)
        rows.append(dtable[at, half].astype(BF16))
    put_slabs(parity_ref, rows, ghost_grad_out)


def add_weights(b, i, sent_ref, received_ref, edges_ref, z_ref, dy_ref, dz_ref, dw1, dw2):
    at = block_at(b)
    z = z_ref[at, :]
    dw2[...] += dot_tn((z * sigmoid(z)).astype(BF16), dy_ref[at, :])
    joined = jnp.concatenate(
        [sent_ref[at, :], received_ref[block_at(i), :], edges_ref[at, :]], axis=1
    )
    dw1[...] += dot_tn(joined, dz_ref[at, :])


def add_shares(b, dz_ref, dsent_ref, send_ref, recv_ref, w1re, edge_grad, dlocal, dtile):
    at = block_at(b)
    back = dot_nt(dz_ref[at, :], w1re).astype(BF16)
    dtile[...] += dot(hits_t(index_row(recv_ref, b), TILE), back[:, :L])
    ids = index_row(send_ref, b)
    upper = column(ids) >= TILE
    dsent32 = dsent_ref[at, :].astype(F32)
    pair = jnp.concatenate(
        [jnp.where(upper, 0.0, dsent32).astype(BF16), jnp.where(upper, dsent32, 0.0).astype(BF16)],
        axis=1,
    )
    dlocal[...] += dot(hits_t(local_index(ids), TILE), pair)
    return edge_grad + back[:, L:].astype(F32)


def pack(dw1, dw2, sums_ref, packed_out):
    gains = sums_ref[512:520, :]
    high = gains.astype(BF16).astype(F32)
    packed_out[0:384, :] = dw1[...].astype(BF16)
    packed_out[384:512, :] = dw2[...].astype(BF16)
    packed_out[512:896, :] = sums_ref[128:512, :].astype(BF16)
    packed_out[896:912, :] = jnp.concatenate([high, gains - high], axis=0).astype(BF16)
    packed_out[912:PACKED, :] = jnp.zeros((PACKED - 912, L), BF16)


def add_partial(partial_ref, dlocal, dtile0, dtile1, partial_out):
    partial_out[0:TILE, :] = partial_ref[0:TILE, :] + dtile0[...] + dlocal[:, :L]
    partial_out[TILE:, :] = partial_ref[TILE:, :] + dtile1[...] + dlocal[:, L:]


def after_kernel(part, layer, sent_ref, received_ref, edges_ref, z_ref, dy_ref, dz_ref, dsent_ref,
                 send_ref, recv_ref, w1_ref, edge_grad_ref, *rest):
    if part:
        dw1_in, dw2_in, dlocal_in, dtile_in, sums_ref, partial_ref = rest[:6]
        edge_grad_out, partial_out, packed_out, dw1, dw2, dlocal, dtile = rest[6:]
        dw1[...] = dw1_in[...]
        dw2[...] = dw2_in[...]
        dlocal[...] = dlocal_in[...]
    else:
        edge_grad_out, dw1, dw2, dlocal, dtile = rest
        dw1[...] = jnp.zeros_like(dw1)
        dw2[...] = jnp.zeros_like(dw2)
        dlocal[...] = jnp.zeros_like(dlocal)
    dtile[...] = jnp.zeros_like(dtile)
    w1re = w1_ref[layer, L:, :]

    def step(i, carry):
        b = i + part * PART_BLOCKS
        add_weights(b, i, sent_ref, received_ref, edges_ref, z_ref, dy_ref, dz_ref, dw1, dw2)
        grad = edge_grad_ref[block_at(b), :].astype(F32)
        grad = add_shares(b, dz_ref, dsent_ref, send_ref, recv_ref, w1re, grad, dlocal, dtile)
        edge_grad_out[block_at(i), :] = grad.astype(BF16)
        return carry

    lax.fori_loop(0, PART_BLOCKS, step, 0, unroll=True)
    if part:
        add_partial(partial_ref, dlocal, dtile_in, dtile, partial_out)
        pack(dw1, dw2, sums_ref, packed_out)


def weights_kernel(sent_ref, received0, received1, edges_ref, z_ref, dy_ref, dz_ref, sums_ref,
                   packed_out, dw1, dw2):
    dw1[...] = jnp.zeros_like(dw1)
    dw2[...] = jnp.zeros_like(dw2)
    for part, received_ref in enumerate((received0, received1)):
        for i in range(PART_BLOCKS):
            add_weights(
                i + part * PART_BLOCKS, i, sent_ref, received_ref, edges_ref, z_ref, dy_ref, dz_ref,
                dw1, dw2
            )
    pack(dw1, dw2, sums_ref, packed_out)


def shares_kernel(dz_ref, dsent_ref, send_ref, recv_ref, w1_ref, edge_grad0, edge_grad1,
                  partial_ref, edge_grad_out, partial_out, dlocal, dtile0, dtile1):
    dlocal[...] = jnp.zeros_like(dlocal)
    w1re = w1_ref[0, L:, :]
    for part, (edge_grad_ref, dtile) in enumerate(((edge_grad0, dtile0), (edge_grad1, dtile1))):
        dtile[...] = jnp.zeros_like(dtile)
        for i in range(PART_BLOCKS):
            b = i + part * PART_BLOCKS
            edge_grad_out[block_at(b), :] = add_shares(
                b, dz_ref, dsent_ref, send_ref, recv_ref, w1re,
                edge_grad_ref[block_at(i), :].astype(F32), dlocal, dtile
            )
    add_partial(partial_ref, dlocal, dtile0, dtile1, partial_out)


def pick_kernel(parity_ref, nodes_ref, ghost_row_ref, *slabs):
    pick(parity_ref, nodes_ref[...], ghost_row_ref, slabs)


def turn_kernel(parity_ref, even_x, odd_x, same, to_even, to_odd):
    rows = [from_both(parity_ref[0, 0] == 0, even_x, odd_x, i) for i in (0, 2)]
    is_even = parity_ref[0, 1] == 0
    left = (rows[0][0], same[0], rows[0][1])
    right = (rows[1][0], same[1], rows[1][1])
    for i in range(3):
        to_even[i] = jnp.where(is_even, right[i], left[i])
        to_odd[i] = jnp.where(is_even, left[i], right[i])


def first_kernel(
    parity_ref, count_ref, nodes_ref, edges_ref, send_ref, recv_ref, ghost_row_ref, w1_ref, w2_ref, g1_ref,
    u1_ref, u2_ref, g2_ref, sent0, z0, sent1, z1, *rest
):
    ghost_refs, rest = rest[:4], rest[4:]
    nodes_out, inbound_out, *slabs = rest[:5]
    outs, (table, inbound) = rest[5:10], rest[10:]
    all_edges_forward(
        parity_ref, count_ref[0, 0], (sent0, z0, sent1, z1), ghost_refs, table, edges_ref, send_ref, recv_ref,
        w1_ref[0, :L, :], w2_ref[0], g1_ref[0:1, :], inbound, outs
    )
    inbound_b = inbound[...].astype(BF16)
    inbound_out[...] = inbound_b
    nodes_next = nodes_forward(nodes_ref[...], inbound_b, u1_ref[0], u2_ref[0], g2_ref[0:1, :])[-1]
    nodes_out[...] = nodes_next
    pick(parity_ref, nodes_next, ghost_row_ref, slabs)


def start_nodes_backward(grad, nodes_b, inbound_b, layer, u1_ref, u2_ref, g2_ref, sums):
    u1, u2, gain = u1_ref[layer], u2_ref[layer], g2_ref[layer : layer + 1, :]
    sums[512:520, :] = jnp.zeros((8, L), F32)
    *saved, nodes_next = nodes_forward(nodes_b, inbound_b, u1, u2, gain)
    through, dinbound = nodes_backward(grad, *saved, u1, u2, gain, sums)
    return nodes_next, grad + through, dinbound


def middle_kernel(
    parity_ref, count_ref, nodes_ref, edges_ref, send_ref, recv_ref, w1_ref, w2_ref, g1_ref, u1_ref, u2_ref,
    g2_ref, node_grad_ref, edge_grad_ref, sent0, z0, sent1, z1, *rest
):
    ghost_refs, rest = rest[:4], rest[4:]
    nodes_out, edges_out, sent_out, z_out, dy_out, dz_out, dsent_out = rest[:7]
    partial_out, sums, *ghost_grad_out = rest[7:12]
    table, inbound, n_all, rstd_all, dinbound, dtable, gain_sum = rest[12:]
    count = count_ref[0, 0]
    w1s, w2, gain = w1_ref[1, :L, :], w2_ref[1], g1_ref[1:2, :]
    all_edges_forward(
        parity_ref, count, (sent0, z0, sent1, z1), ghost_refs, table, edges_ref, send_ref, recv_ref, w1s, w2,
        gain, inbound, (edges_out, sent_out, z_out, n_all, rstd_all)
    )
    nodes_out[...], partial_out[...], dinbound[...] = start_nodes_backward(
        node_grad_ref[...].astype(F32), nodes_ref[...], inbound[...].astype(BF16), 1, u1_ref,
        u2_ref, g2_ref, sums
    )
    all_edges_backward(
        parity_ref, count, edge_grad_ref, dinbound, (z_out, n_all, rstd_all), send_ref, recv_ref, w1s, w2, gain,
        (dy_out, dz_out, dsent_out), gain_sum, dtable, ghost_grad_out
    )
    sums[512:513, :] = gain_sum[0:1, :]


def last_kernel(
    parity_ref, count_ref, nodes_ref, inbound_ref, send_ref, recv_ref, ghost_row_ref, w1_ref, w2_ref, g1_ref,
    u1_ref, u2_ref, g2_ref, partial_ref, edge_grad0_ref, edge_grad1_ref, z_ref, n_ref, rstd_ref,
    *rest
):
    returned_refs, rest = rest[:4], rest[4:]
    dy_out, dz_out, dsent_out, partial_out, sums, *ghost_grad_out = rest[:8]
    dinbound, dtable, gain_sum, edge_grad = rest[8:]
    node_grad = add_returned(parity_ref, partial_ref[...], returned_refs, ghost_row_ref)
    _, partial_out[...], dinbound[...] = start_nodes_backward(
        node_grad.astype(BF16).astype(F32), nodes_ref[...], inbound_ref[...], 0, u1_ref, u2_ref,
        g2_ref, sums
    )
    edge_grad[0:PART, :] = edge_grad0_ref[...]
    edge_grad[PART:, :] = edge_grad1_ref[...]
    all_edges_backward(
        parity_ref, count_ref[0, 0], edge_grad, dinbound, (z_ref, n_ref, rstd_ref), send_ref, recv_ref,
        w1_ref[0, :L, :], w2_ref[0], g1_ref[0:1, :], (dy_out, dz_out, dsent_out), gain_sum, dtable,
        ghost_grad_out
    )
    sums[512:513, :] = gain_sum[0:1, :]


def add_returned(parity_ref, partial, returned_refs, ghost_row_ref):
    row = jnp.concatenate([ghost_row_ref[i, j : j + 1, :] for i, j in OUTER], axis=1)
    returned = jnp.concatenate(arrived(parity_ref, returned_refs), axis=0)
    return partial + dot(hits_t(row, NODES), returned)


def return_kernel(parity_ref, partial_ref, ghost_row_ref, *rest):
    rest[4][...] = add_returned(parity_ref, partial_ref[...], rest[:4], ghost_row_ref)


def call(kernel, name, outs, scratch, scalars, flops, *args):
    vmem = pl.BlockSpec(memory_space=pltpu.VMEM)
    smem = pl.BlockSpec(memory_space=pltpu.SMEM)
    return pl.pallas_call(
        kernel,
        name=name,
        out_shape=[jax.ShapeDtypeStruct(s, d) for s, d in outs],
        in_specs=[smem] * scalars + [vmem] * (len(args) - scalars),
        out_specs=[vmem] * len(outs),
        scratch_shapes=[pltpu.VMEM(s, d) for s, d in scratch],
        cost_estimate=pl.CostEstimate(flops=flops, bytes_accessed=1 << 20, transcendentals=0),
        compiler_params=pltpu.CompilerParams(vmem_limit_bytes=24 * 1024 * 1024),
    )(*args)


def swap(axis, to_even, to_odd):
    def pairs(first):
        ups = [(i, i + 1) for i in range(first, lax.axis_size(axis) - 1, 2)]
        return ups + [(j, i) for i, j in ups]

    odd = lax.ppermute(to_odd, axis, pairs(1))
    return lax.ppermute(to_even, axis, pairs(0)), odd


def turn(parity, even_x, odd_x, same):
    outs = [(even_x.shape, BF16)] * 2
    return call(turn_kernel, "turn", outs, [], 1, 10**6, parity, even_x, odd_x, same)


def exchange(parity, slabs, beside):
    to_even, to_odd, same = slabs
    even_x, odd_x = swap("gx", to_even, to_odd)
    first = beside(0, None)
    to_even, to_odd = turn(parity, even_x, odd_x, same)
    even_y, odd_y = swap("gy", to_even, to_odd)
    second = beside(1, (first, to_even))
    return (even_x, odd_x, even_y, odd_y), first, second


def sum_over_domains(packed, parity, slabs, late):
    axes = ("gx", "gy")
    plane, line = planes_and_lines(lax.axis_size("gx"), lax.axis_size("gy"))
    hold = lax.optimization_barrier

    def trade(parts, groups):
        return lax.all_to_all(parts, axes, 0, 0, tiled=True, axis_index_groups=groups)

    def copies(parts, groups):
        mine = jnp.sum(parts.astype(F32), axis=0).astype(BF16)
        return jnp.broadcast_to(mine[None], (len(groups[0]),) + mine.shape)

    to_even, to_odd, same = slabs
    packed, to_even, to_odd = hold((packed.reshape(len(plane[0]), -1, L), to_even, to_odd))
    parts = trade(packed, plane)
    parts, even_x, odd_x = hold((parts, *swap("gx", to_even, to_odd)))
    parts, same = hold((copies(parts, line), same))
    parts = trade(parts, line)
    parts, even_y, odd_y = hold((parts, *swap("gy", *turn(parity, even_x, odd_x, same))))
    parts, late = hold((copies(parts, plane), late))
    total = trade(parts, plane).reshape(LAYERS, PACKED, L)
    return total, (even_x, odd_x, even_y, odd_y), late


def planes_and_lines(rows, columns):
    planes, lines = {}, {}
    for i in range(rows * columns):
        gx, gy = divmod(i, columns)
        y, z_low = divmod(gx, 4)
        z_high, rest = divmod(gy, 8)
        planes.setdefault((z_high, z_low), []).append(i)
        lines.setdefault((y, rest), []).append(i)
    return list(planes.values()), list(lines.values())


def unpack_kernel(total_ref, dw1, dw2, dg1, du1, du2, dg2):
    for i in range(LAYERS):
        dw1[i] = total_ref[i, 0:384, :].astype(F32)
        dw2[i] = total_ref[i, 384:512, :].astype(F32)
        du1[i] = total_ref[i, 512:768, :].astype(F32)
        du2[i] = total_ref[i, 768:896, :].astype(F32)
        gains = total_ref[i, 896:912, :].astype(F32)
        dg1[i : i + 1, :] = gains[0:1, :] + gains[8:9, :]
        dg2[i : i + 1, :] = gains[1:2, :] + gains[9:10, :]


def on_device(
    latents,
    edge_latents,
    senders,
    receivers,
    ghost_rows,
    edge_count,
    node_cotangent,
    edge_cotangent,
    edge_first,
    edge_second,
    edge_scale,
    node_first,
    node_second,
    node_scale,
):
    nodes0 = latents[0, 0]
    parity = jnp.stack([lax.axis_index(axis) % 2 for axis in ("gx", "gy")])[None]
    edges0 = edge_latents[0, 0]
    ids = senders[0]
    targets = receivers[0]
    grow = ghost_rows[0, 0]
    weights = (edge_first, edge_second, edge_scale, node_first, node_second, node_scale)

    node_b = ((NODES, L), BF16)
    node_f = ((NODES, L), F32)
    edge_b = ((EDGES, L), BF16)
    edge_f = ((EDGES, L), F32)
    part_b = ((PART, L), BF16)
    part_f = ((PART, L), F32)
    slabs_b = [((n, G, L), BF16) for n in (3, 3, 2)]
    packed_b = ((PACKED, L), BF16)
    sums_f = ((520, L), F32)
    pair_b = ((NODES, 2 * L), BF16)
    pair_f = ((NODES, 2 * L), F32)
    gain_f = ((8, L), F32)
    dw1_f = ((3 * L, L), F32)
    dw2_f = ((L, L), F32)
    dlocal_f = ((TILE, 2 * L), F32)
    dtile_f = ((TILE, L), F32)

    def before(layer, nodes, edges):
        def part_of(part, wait):
            node_arg = nodes
            if wait is not None:
                node_arg, _ = lax.optimization_barrier((nodes, wait))
            return call(
                functools.partial(before_kernel, part, layer), f"before{layer}{part}",
                [part_b, part_b, part_f], [], 0, 2 * 10**9, node_arg, edges, ids, targets,
                edge_first
            )

        return part_of

    def after(layer, sent, received, edges, z, dy, dz, dsent, edge_grads, sums, partial):
        def part_of(part, wait):
            dy_arg, extra = dy, ()
            if part:
                dy_arg, _ = lax.optimization_barrier((dy, wait[1]))
                extra = (*wait[0][1:], sums, partial)
            outs = [part_b]
            outs += [node_f, packed_b] if part else [dw1_f, dw2_f, dlocal_f, dtile_f]
            return call(
                functools.partial(after_kernel, part, layer), f"after{layer}{part}", outs,
                [dw1_f, dw2_f, dlocal_f, dtile_f] if part else [], 0, 2 * 10**9, sent,
                received[part], edges, z, dy_arg, dz, dsent, ids, targets, edge_first, edge_grads,
                *extra
            )

        return part_of

    picked = call(pick_kernel, "pick", slabs_b, [], 1, 10**8, parity, nodes0, grow)
    ghosts, a0, a1 = exchange(parity, picked, before(0, nodes0, edges0))
    nodes1, inbound, *picked, edges1, sent_0, z_0, n_0, rstd_0 = call(
        first_kernel, "first", [node_b, node_b, *slabs_b, edge_b, edge_b, edge_f, edge_f, edge_f],
        [pair_b, node_f], 2, 4 * 10**9, parity, edge_count, nodes0, edges0, ids, targets, grow, *weights,
        a0[0], a0[2], a1[0], a1[2], *ghosts
    )
    received_0 = (a0[1], a1[1])
    ghosts, a0, a1 = exchange(parity, picked, before(1, nodes1, edges1))
    received_1 = (a0[1], a1[1])
    nodes2, edges2, sent_1, z_1, dy, dz, dsent, partial, sums, *ghost_grad = call(
        middle_kernel, "middle",
        [node_b, edge_b, edge_b, edge_f, edge_b, edge_b, edge_b, node_f, sums_f, *slabs_b],
        [pair_b, node_f, edge_f, edge_f, node_b, pair_f, gain_f], 2, 8 * 10**9, parity, edge_count, nodes1,
        edges1, ids, targets, *weights, node_cotangent[0, 0], edge_cotangent[0, 0], a0[0], a0[2],
        a1[0], a1[2], *ghosts
    )
    returned, c0, c1 = exchange(
        parity, ghost_grad,
        after(1, sent_1, received_1, edges1, z_1, dy, dz, dsent, edge_cotangent[0, 0], sums, partial),
    )
    edge_grad0, (edge_grad1, partial, packed1) = c0[0], c1
    dy, dz, dsent, partial, sums, *ghost_grad = call(
        last_kernel, "last", [edge_b, edge_b, edge_b, node_f, sums_f, *slabs_b],
        [node_b, pair_f, gain_f, edge_b], 2, 4 * 10**9, parity, edge_count, nodes0, inbound, ids, targets,
        grow, *weights, partial, edge_grad0, edge_grad1, z_0, n_0, rstd_0, *returned
    )
    (packed0,) = call(
        weights_kernel, "weights", [packed_b], [dw1_f, dw2_f], 0, 2 * 10**9, sent_0, *received_0,
        edges0, z_0, dy, dz, sums
    )
    packed = jnp.concatenate([packed0, packed1], axis=0)
    total, returned, dsent = sum_over_domains(packed, parity, ghost_grad, dsent)
    edge_grad, partial = call(
        shares_kernel, "shares", [edge_f, node_f], [dlocal_f, dtile_f, dtile_f], 0, 2 * 10**9, dz,
        dsent, ids, targets, edge_first, edge_grad0, edge_grad1, partial
    )
    (node_grad,) = call(
        return_kernel, "returned", [node_f], [], 1, 10**8, parity, partial, grow, *returned
    )
    grads = call(
        unpack_kernel, "unpack", [((LAYERS,) + w.shape[1:], F32) for w in weights], [], 0, 10**6,
        total
    )
    return (
        nodes2[None, None],
        edges2[None, None],
        node_grad[None, None],
        edge_grad[None, None],
        *grads,
    )


def solution(mesh):
    domain = P("gx", "gy", None, None)
    placed = (
        domain,
        domain,
        P("gx", "gy", None),
        P("gx", "gy", None),
        P("gx", "gy", None, None, None),
        P("gx", "gy"),
        domain,
        domain,
        P(),
        P(),
        P(),
        P(),
        P(),
        P(),
    )
    return jax.shard_map(
        on_device,
        mesh=mesh,
        in_specs=placed,
        out_specs=(domain, domain, domain, domain, P(), P(), P(), P(), P(), P()),
        check_vma=False,
    )
```

```python
import functools

import jax
import jax.numpy as jnp
from jax import lax
from jax.experimental import pallas as pl
from jax.experimental.pallas import tpu as pltpu
from jax.sharding import PartitionSpec as P

L = 128
LAYERS = 2
TILE = 256
DEG = 8
G = 128
NODES = 512
EDGES = 4096
PART = TILE * DEG
BLOCK = 1024
BLOCKS = EDGES // BLOCK
PART_BLOCKS = PART // BLOCK
PACKED = 1024
OUTER = ((0, 0), (0, 1), (0, 2), (1, 0), (1, 2), (2, 0), (2, 1), (2, 2))

F32 = jnp.float32
BF16 = jnp.bfloat16
epsilon = 1e-05


def dot(a, b):
    return jnp.dot(a, b, preferred_element_type=F32)


def dot_nt(a, b):
    return lax.dot_general(a, b, (((1,), (1,)), ((), ())), preferred_element_type=F32)


def dot_tn(a, b):
    return lax.dot_general(a, b, (((0,), (0,)), ((), ())), preferred_element_type=F32)


def sigmoid(v):
    return 0.5 * jnp.tanh(0.5 * v) + 0.5


def column(row):
    parts = [
        jnp.transpose(jnp.broadcast_to(row[:, i : i + 128], (128, 128)))
        for i in range(0, row.shape[1], 128)
    ]
    return jnp.concatenate(parts, axis=0) if len(parts) > 1 else parts[0]


def hits(col, width):
    lane = lax.broadcasted_iota(jnp.int32, col.shape, 1)
    parts = [
        jnp.where(col == lane + 128 * t, 1.0, 0.0).astype(BF16) for t in range(width // 128)
    ]
    return jnp.concatenate(parts, axis=1)


def hits_t(row, height):
    sub = lax.broadcasted_iota(jnp.int32, (height, row.shape[1]), 0)
    return jnp.where(sub == row, 1.0, 0.0).astype(BF16)


def layer_norm(y):
    center = y - jnp.mean(y, axis=-1, keepdims=True)
    spread = jnp.mean(center * center, axis=-1, keepdims=True)
    rstd = lax.rsqrt(spread + epsilon)
    return center * rstd, rstd


def layer_norm_grad(dn, n, rstd):
    return rstd * (
        dn
        - jnp.mean(dn, axis=-1, keepdims=True)
        - n * jnp.mean(dn * n, axis=-1, keepdims=True)
    )


def silu_grad(z):
    s = sigmoid(z)
    return s * (1.0 + z * (1.0 - s))


def block_at(b):
    return pl.ds(pl.multiple_of(b * BLOCK, BLOCK), BLOCK)


def tile_at(b):
    return pl.ds(pl.multiple_of((b // PART_BLOCKS) * TILE, TILE), TILE)


def index_row(ref, b):
    return ref[:, block_at(b)]


def local_index(ids):
    return jnp.where(ids < TILE, ids, jnp.where(ids < NODES, ids - TILE, -1))


def ghost_index(ids):
    g = ids - NODES
    g = jnp.where(g >= 4 * G, g - G, g)
    return jnp.where(g >= NODES, g - NODES, g)


def ghost_upper(ids):
    return ids >= NODES + NODES + G


def live_of(b, count):
    slot = lax.broadcasted_iota(jnp.int32, (BLOCK, L), 0) + b * BLOCK
    return jnp.where(slot < count, 1.0, 0.0)


def pick(nodes_b, ghost_row_ref, slabs):
    rows = []
    for i, j in OUTER:
        col = column(ghost_row_ref[i, j : j + 1, :])
        rows.append(dot(hits(col, NODES), nodes_b).astype(BF16))
    put_slabs(rows, slabs)


def even_on(axis):
    return lax.rem(lax.axis_index(axis), 2) == 0


def put_slabs(rows, slabs):
    to_even, to_odd, same = slabs
    is_even = even_on("gx")
    for i in range(3):
        to_even[i] = jnp.where(is_even, rows[5 + i], rows[i])
        to_odd[i] = jnp.where(is_even, rows[i], rows[5 + i])
    same[0] = rows[3]
    same[1] = rows[4]


def from_both(is_even, even_ref, odd_ref, i):
    even, odd = even_ref[i], odd_ref[i]
    return jnp.where(is_even, odd, even), jnp.where(is_even, even, odd)


def arrived(refs):
    even_x, odd_x, even_y, odd_y = refs
    row = from_both(even_on("gx"), even_x, odd_x, 1)
    columns = [from_both(even_on("gy"), even_y, odd_y, i) for i in range(3)]
    return [
        columns[0][0], row[0], columns[0][1], columns[1][0], columns[1][1], columns[2][0], row[1],
        columns[2][1]
    ]


def local_pair(nodes_ref):
    return jnp.concatenate([nodes_ref[0:TILE, :], nodes_ref[TILE:NODES, :]], axis=1)


def ghost_pair(ghost_refs):
    rows = arrived(ghost_refs)
    lower = jnp.concatenate(rows[:4], axis=0)
    upper = jnp.concatenate(rows[4:], axis=0)
    return jnp.concatenate([lower, upper], axis=1)


def nodes_forward(nodes_b, inbound_b, u1, u2, gain):
    joined = jnp.concatenate([nodes_b, inbound_b], axis=1)
    z = dot(joined, u1)
    hidden = (z * sigmoid(z)).astype(BF16)
    n, rstd = layer_norm(dot(hidden, u2))
    nodes_next = (nodes_b.astype(F32) + n * gain).astype(BF16)
    return joined, z, hidden, n, rstd, nodes_next


def nodes_backward(grad, joined, z, hidden, n, rstd, u1, u2, gain, sums):
    sums[384:512, :] = dot_tn(hidden, (dy := layer_norm_grad(grad * gain, n, rstd).astype(BF16)))
    sums[513:514, :] = jnp.sum(grad * n, axis=0, keepdims=True)
    dz = (dot_nt(dy, u2).astype(BF16).astype(F32) * silu_grad(z)).astype(BF16)
    sums[128:384, :] = dot_tn(joined, dz)
    back = dot_nt(dz, u1).astype(BF16)
    return back[:, :L].astype(F32), back[:, L:]


def before_kernel(part, layer, nodes_ref, edges_ref, send_ref, recv_ref, w1_ref, sent_out,
                  received_out, z_out):
    pair = local_pair(nodes_ref)
    tile = nodes_ref[part * TILE : (part + 1) * TILE, :]
    w1 = w1_ref[layer]

    def step(i, carry):
        b = i + part * PART_BLOCKS
        ids = index_row(send_ref, b)
        both = dot(hits(column(local_index(ids)), TILE), pair)
        sent = jnp.where(column(ids) >= TILE, both[:, L:], both[:, :L]).astype(BF16)
        received = dot(hits(column(index_row(recv_ref, b)), TILE), tile).astype(BF16)
        sent_out[block_at(i), :] = sent
        received_out[block_at(i), :] = received
        joined = jnp.concatenate([sent, received, edges_ref[block_at(b), :]], axis=1)
        z_out[block_at(i), :] = dot(joined, w1)
        return carry

    lax.fori_loop(0, PART_BLOCKS, step, 0)


def edges_forward(b, local, count, table, edges_ref, send_ref, recv_ref, w1s, w2, gain, inbound,
                  edges_out, sent_out, z_out, n_out, rstd_out):
    sent_ref, z_ref, i = local
    ids = index_row(send_ref, b)
    both = dot(hits(column(ghost_index(ids)), NODES), table)
    sent = jnp.where(column(ids) >= 2 * NODES + G, both[:, L:], both[:, :L]).astype(BF16)
    z = z_ref[block_at(i), :] + dot(sent, w1s)
    hidden = (z * sigmoid(z)).astype(BF16)
    n, rstd = layer_norm(dot(hidden, w2))
    message = n * gain * live_of(b, count)
    at = block_at(b)
    edges_out[at, :] = (edges_ref[at, :].astype(F32) + message).astype(BF16)
    inbound[tile_at(b), :] += dot(hits_t(index_row(recv_ref, b), TILE), message.astype(BF16))
    sent_out[at, :] = sent_ref[block_at(i), :] + sent
    z_out[at, :] = z
    n_out[at, :] = n
    rstd_out[at, :] = jnp.broadcast_to(rstd, (BLOCK, L))


def all_edges_forward(count, locals_, ghost_refs, table, edges_ref, send_ref, recv_ref, w1s, w2,
                      gain, inbound, outs):
    table[...] = ghost_pair(ghost_refs)
    inbound[...] = jnp.zeros_like(inbound)
    for part in range(2):
        sent_ref, z_ref = locals_[2 * part : 2 * part + 2]

        def step(i, carry, part=part, sent_ref=sent_ref, z_ref=z_ref):
            edges_forward(
                i + part * PART_BLOCKS, (sent_ref, z_ref, i), count, table[...], edges_ref,
                send_ref, recv_ref, w1s, w2, gain, inbound, *outs
            )
            return carry

        lax.fori_loop(0, PART_BLOCKS, step, 0, unroll=True)


def edges_backward(b, count, grad_ref, dinbound, z_ref, n_ref, rstd_ref, send_ref, recv_ref, w1s,
                   w2, gain, dy_out, dz_out, dsent_out, gain_sum, dtable):
    at = block_at(b)
    n = n_ref[at, :]
    from_nodes = dot(hits(column(index_row(recv_ref, b)), TILE), dinbound[tile_at(b), :])
    dmessage = (grad_ref[at, :].astype(F32) + from_nodes) * live_of(b, count)
    gain_sum[0:1, :] += jnp.sum(dmessage * n, axis=0, keepdims=True)
    dy = layer_norm_grad(dmessage * gain, n, rstd_ref[at, :]).astype(BF16)
    dz = (dot_nt(dy, w2).astype(BF16).astype(F32) * silu_grad(z_ref[at, :])).astype(BF16)
    dsent = dot_nt(dz, w1s).astype(BF16)
    dy_out[at, :] = dy
    dz_out[at, :] = dz
    dsent_out[at, :] = dsent
    ids = index_row(send_ref, b)
    upper = column(ids) >= 2 * NODES + G
    dsent32 = dsent.astype(F32)
    pair = jnp.concatenate(
        [jnp.where(upper, 0.0, dsent32).astype(BF16), jnp.where(upper, dsent32, 0.0).astype(BF16)],
        axis=1,
    )
    dtable[...] += dot(hits_t(ghost_index(ids), NODES), pair)


def all_edges_backward(count, grad_ref, dinbound, residuals, send_ref, recv_ref, w1s, w2, gain,
                       outs, gain_sum, dtable, ghost_grad_out):
    gain_sum[...] = jnp.zeros_like(gain_sum)
    dtable[...] = jnp.zeros_like(dtable)

    def step(b, carry):
        edges_backward(
            b, count, grad_ref, dinbound, *residuals, send_ref, recv_ref, w1s, w2, gain, *outs,
            gain_sum, dtable
        )
        return carry

    lax.fori_loop(0, BLOCKS, step, 0, unroll=True)
    rows = []
    for s in range(8):
        at, half = pl.ds((s % 4) * G, G), pl.ds((s // 4) * L, L)
        rows.append(dtable[at, half].astype(BF16))
    put_slabs(rows, ghost_grad_out)


def add_weights(b, i, sent_ref, received_ref, edges_ref, z_ref, dy_ref, dz_ref, dw1, dw2):
    at = block_at(b)
    z = z_ref[at, :]
    dw2[...] += dot_tn((z * sigmoid(z)).astype(BF16), dy_ref[at, :])
    joined = jnp.concatenate(
        [sent_ref[at, :], received_ref[block_at(i), :], edges_ref[at, :]], axis=1
    )
    dw1[...] += dot_tn(joined, dz_ref[at, :])


def add_shares(b, dz_ref, dsent_ref, send_ref, recv_ref, w1re, edge_grad, dlocal, dtile):
    at = block_at(b)
    back = dot_nt(dz_ref[at, :], w1re).astype(BF16)
    dtile[...] += dot(hits_t(index_row(recv_ref, b), TILE), back[:, :L])
    ids = index_row(send_ref, b)
    upper = column(ids) >= TILE
    dsent32 = dsent_ref[at, :].astype(F32)
    pair = jnp.concatenate(
        [jnp.where(upper, 0.0, dsent32).astype(BF16), jnp.where(upper, dsent32, 0.0).astype(BF16)],
        axis=1,
    )
    dlocal[...] += dot(hits_t(local_index(ids), TILE), pair)
    return edge_grad + back[:, L:].astype(F32)


def pack(dw1, dw2, sums_ref, packed_out):
    gains = sums_ref[512:520, :]
    high = gains.astype(BF16).astype(F32)
    packed_out[0:384, :] = dw1[...].astype(BF16)
    packed_out[384:512, :] = dw2[...].astype(BF16)
    packed_out[512:896, :] = sums_ref[128:512, :].astype(BF16)
    packed_out[896:912, :] = jnp.concatenate([high, gains - high], axis=0).astype(BF16)
    packed_out[912:PACKED, :] = jnp.zeros((PACKED - 912, L), BF16)


def add_partial(partial_ref, dlocal, dtile0, dtile1, partial_out):
    partial_out[0:TILE, :] = partial_ref[0:TILE, :] + dtile0[...] + dlocal[:, :L]
    partial_out[TILE:, :] = partial_ref[TILE:, :] + dtile1[...] + dlocal[:, L:]


def after_kernel(part, layer, sent_ref, received_ref, edges_ref, z_ref, dy_ref, dz_ref, dsent_ref,
                 send_ref, recv_ref, w1_ref, edge_grad_ref, *rest):
    if part:
        dw1_in, dw2_in, dlocal_in, dtile_in, sums_ref, partial_ref = rest[:6]
        edge_grad_out, partial_out, packed_out, dw1, dw2, dlocal, dtile = rest[6:]
        dw1[...] = dw1_in[...]
        dw2[...] = dw2_in[...]
        dlocal[...] = dlocal_in[...]
    else:
        edge_grad_out, dw1, dw2, dlocal, dtile = rest
        dw1[...] = jnp.zeros_like(dw1)
        dw2[...] = jnp.zeros_like(dw2)
        dlocal[...] = jnp.zeros_like(dlocal)
    dtile[...] = jnp.zeros_like(dtile)
    w1re = w1_ref[layer, L:, :]

    def step(i, carry):
        b = i + part * PART_BLOCKS
        add_weights(b, i, sent_ref, received_ref, edges_ref, z_ref, dy_ref, dz_ref, dw1, dw2)
        grad = edge_grad_ref[block_at(b), :].astype(F32)
        grad = add_shares(b, dz_ref, dsent_ref, send_ref, recv_ref, w1re, grad, dlocal, dtile)
        edge_grad_out[block_at(i), :] = grad.astype(BF16)
        return carry

    lax.fori_loop(0, PART_BLOCKS, step, 0)
    if part:
        add_partial(partial_ref, dlocal, dtile_in, dtile, partial_out)
        pack(dw1, dw2, sums_ref, packed_out)


def weights_kernel(sent_ref, received0, received1, edges_ref, z_ref, dy_ref, dz_ref, sums_ref,
                   packed1_ref, packed_out, dw1, dw2):
    dw1[...] = jnp.zeros_like(dw1)
    dw2[...] = jnp.zeros_like(dw2)
    for part, received_ref in enumerate((received0, received1)):
        for i in range(PART_BLOCKS):
            add_weights(
                i + part * PART_BLOCKS, i, sent_ref, received_ref, edges_ref, z_ref, dy_ref, dz_ref,
                dw1, dw2
            )
    pack(dw1, dw2, sums_ref, packed_out)
    packed_out[PACKED:, :] = packed1_ref[...]


def shares_kernel(dz_ref, dsent_ref, send_ref, recv_ref, w1_ref, edge_grad0, edge_grad1,
                  partial_ref, edge_grad_out, partial_out, dlocal, dtile0, dtile1):
    dlocal[...] = jnp.zeros_like(dlocal)
    w1re = w1_ref[0, L:, :]
    for part, (edge_grad_ref, dtile) in enumerate(((edge_grad0, dtile0), (edge_grad1, dtile1))):
        dtile[...] = jnp.zeros_like(dtile)

        def step(i, carry, part=part, edge_grad_ref=edge_grad_ref, dtile=dtile):
            b = i + part * PART_BLOCKS
            edge_grad_out[block_at(b), :] = add_shares(
                b, dz_ref, dsent_ref, send_ref, recv_ref, w1re,
                edge_grad_ref[block_at(i), :].astype(F32), dlocal, dtile
            )
            return carry

        lax.fori_loop(0, PART_BLOCKS, step, 0)
    add_partial(partial_ref, dlocal, dtile0, dtile1, partial_out)


def pick_kernel(nodes_ref, ghost_row_ref, *slabs):
    pick(nodes_ref[...], ghost_row_ref, slabs)


def turn_kernel(even_x, odd_x, same, to_even, to_odd):
    rows = [from_both(even_on("gx"), even_x, odd_x, i) for i in (0, 2)]
    is_even = even_on("gy")
    left = (rows[0][0], same[0], rows[0][1])
    right = (rows[1][0], same[1], rows[1][1])
    for i in range(3):
        to_even[i] = jnp.where(is_even, right[i], left[i])
        to_odd[i] = jnp.where(is_even, left[i], right[i])


def first_kernel(
    count_ref, nodes_ref, edges_ref, send_ref, recv_ref, ghost_row_ref, w1_ref, w2_ref, g1_ref,
    u1_ref, u2_ref, g2_ref, sent0, z0, sent1, z1, *rest
):
    ghost_refs, rest = rest[:4], rest[4:]
    nodes_out, inbound_out, *slabs = rest[:5]
    outs, (table, inbound) = rest[5:10], rest[10:]
    all_edges_forward(
        count_ref[0, 0], (sent0, z0, sent1, z1), ghost_refs, table, edges_ref, send_ref, recv_ref,
        w1_ref[0, :L, :], w2_ref[0], g1_ref[0:1, :], inbound, outs
    )
    inbound_b = inbound[...].astype(BF16)
    inbound_out[...] = inbound_b
    nodes_next = nodes_forward(nodes_ref[...], inbound_b, u1_ref[0], u2_ref[0], g2_ref[0:1, :])[-1]
    nodes_out[...] = nodes_next
    pick(nodes_next, ghost_row_ref, slabs)


def start_nodes_backward(grad, nodes_b, inbound_b, layer, u1_ref, u2_ref, g2_ref, sums):
    u1, u2, gain = u1_ref[layer], u2_ref[layer], g2_ref[layer : layer + 1, :]
    sums[512:520, :] = jnp.zeros((8, L), F32)
    *saved, nodes_next = nodes_forward(nodes_b, inbound_b, u1, u2, gain)
    through, dinbound = nodes_backward(grad, *saved, u1, u2, gain, sums)
    return nodes_next, grad + through, dinbound


def middle_kernel(
    count_ref, nodes_ref, edges_ref, send_ref, recv_ref, w1_ref, w2_ref, g1_ref, u1_ref, u2_ref,
    g2_ref, node_grad_ref, edge_grad_ref, sent0, z0, sent1, z1, *rest
):
    ghost_refs, rest = rest[:4], rest[4:]
    nodes_out, edges_out, sent_out, z_out, dy_out, dz_out, dsent_out = rest[:7]
    partial_out, sums, *ghost_grad_out = rest[7:12]
    table, inbound, n_all, rstd_all, dinbound, dtable, gain_sum = rest[12:]
    count = count_ref[0, 0]
    w1s, w2, gain = w1_ref[1, :L, :], w2_ref[1], g1_ref[1:2, :]
    all_edges_forward(
        count, (sent0, z0, sent1, z1), ghost_refs, table, edges_ref, send_ref, recv_ref, w1s, w2,
        gain, inbound, (edges_out, sent_out, z_out, n_all, rstd_all)
    )
    nodes_out[...], partial_out[...], dinbound[...] = start_nodes_backward(
        node_grad_ref[...].astype(F32), nodes_ref[...], inbound[...].astype(BF16), 1, u1_ref,
        u2_ref, g2_ref, sums
    )
    all_edges_backward(
        count, edge_grad_ref, dinbound, (z_out, n_all, rstd_all), send_ref, recv_ref, w1s, w2, gain,
        (dy_out, dz_out, dsent_out), gain_sum, dtable, ghost_grad_out
    )
    sums[512:513, :] = gain_sum[0:1, :]


def last_kernel(
    count_ref, nodes_ref, inbound_ref, send_ref, recv_ref, ghost_row_ref, w1_ref, w2_ref, g1_ref,
    u1_ref, u2_ref, g2_ref, partial_ref, edge_grad0_ref, edge_grad1_ref, z_ref, n_ref, rstd_ref,
    *rest
):
    returned_refs, rest = rest[:4], rest[4:]
    dy_out, dz_out, dsent_out, partial_out, sums, *ghost_grad_out = rest[:8]
    dinbound, dtable, gain_sum, edge_grad = rest[8:]
    node_grad = add_returned(partial_ref[...], returned_refs, ghost_row_ref)
    _, partial_out[...], dinbound[...] = start_nodes_backward(
        node_grad.astype(BF16).astype(F32), nodes_ref[...], inbound_ref[...], 0, u1_ref, u2_ref,
        g2_ref, sums
    )
    edge_grad[0:PART, :] = edge_grad0_ref[...]
    edge_grad[PART:, :] = edge_grad1_ref[...]
    all_edges_backward(
        count_ref[0, 0], edge_grad, dinbound, (z_ref, n_ref, rstd_ref), send_ref, recv_ref,
        w1_ref[0, :L, :], w2_ref[0], g1_ref[0:1, :], (dy_out, dz_out, dsent_out), gain_sum, dtable,
        ghost_grad_out
    )
    sums[512:513, :] = gain_sum[0:1, :]


def add_returned(partial, returned_refs, ghost_row_ref):
    row = jnp.concatenate([ghost_row_ref[i, j : j + 1, :] for i, j in OUTER], axis=1)
    returned = jnp.concatenate(arrived(returned_refs), axis=0)
    return partial + dot(hits_t(row, NODES), returned)


def return_kernel(partial_ref, ghost_row_ref, *rest):
    rest[4][...] = add_returned(partial_ref[...], rest[:4], ghost_row_ref)


def call(kernel, name, outs, scratch, scalars, flops, *args):
    vmem = pl.BlockSpec(memory_space=pltpu.VMEM)
    smem = pl.BlockSpec(memory_space=pltpu.SMEM)
    return pl.pallas_call(
        kernel,
        name=name,
        out_shape=[jax.ShapeDtypeStruct(s, d) for s, d in outs],
        in_specs=[smem] * scalars + [vmem] * (len(args) - scalars),
        out_specs=[vmem] * len(outs),
        scratch_shapes=[pltpu.VMEM(s, d) for s, d in scratch],
        cost_estimate=pl.CostEstimate(flops=flops, bytes_accessed=1 << 20, transcendentals=0),
        compiler_params=pltpu.CompilerParams(vmem_limit_bytes=24 * 1024 * 1024),
    )(*args)


def swap(axis, to_even, to_odd):
    def pairs(first):
        ups = [(i, i + 1) for i in range(first, lax.axis_size(axis) - 1, 2)]
        return ups + [(j, i) for i, j in ups]

    odd = lax.ppermute(to_odd, axis, pairs(1))
    return lax.ppermute(to_even, axis, pairs(0)), odd


def turn(even_x, odd_x, same):
    outs = [(even_x.shape, BF16)] * 2
    return call(turn_kernel, "turn", outs, [], 0, 10**6, even_x, odd_x, same)


def exchange(slabs, beside):
    to_even, to_odd, same = slabs
    even_x, odd_x = swap("gx", to_even, to_odd)
    first = beside(0, None)
    to_even, to_odd = turn(even_x, odd_x, same)
    even_y, odd_y = swap("gy", to_even, to_odd)
    second = beside(1, (first, to_even))
    return (even_x, odd_x, even_y, odd_y), first, second


def sum_over_domains(packed, slabs, late):
    axes = ("gx", "gy")
    plane, line = planes_and_lines(lax.axis_size("gx"), lax.axis_size("gy"))
    hold = lax.optimization_barrier

    def trade(parts, groups):
        return lax.all_to_all(parts, axes, 0, 0, tiled=True, axis_index_groups=groups)

    def copies(parts, groups):
        shape = (len(groups[0]),) + parts.shape[1:]
        return call(spread_kernel, "spread", [(shape, BF16)], [], 0, 10**6, parts)[0]

    to_even, to_odd, same = slabs
    packed, to_even, to_odd = hold((packed.reshape(len(plane[0]), -1, L), to_even, to_odd))
    parts = trade(packed, plane)
    parts, even_x, odd_x = hold((parts, *swap("gx", to_even, to_odd)))
    parts, same = hold((copies(parts, line), same))
    parts = trade(parts, line)
    parts, even_y, odd_y = hold((parts, *swap("gy", *turn(even_x, odd_x, same))))
    parts, late = hold((copies(parts, plane), late))
    total = trade(parts, plane).reshape(LAYERS, PACKED, L)
    return total, (even_x, odd_x, even_y, odd_y), late


def planes_and_lines(rows, columns):
    planes, lines = {}, {}
    for i in range(rows * columns):
        gx, gy = divmod(i, columns)
        y, z_low = divmod(gx, 4)
        z_high, rest = divmod(gy, 8)
        planes.setdefault((z_high, z_low), []).append(i)
        lines.setdefault((y, rest), []).append(i)
    return list(planes.values()), list(lines.values())


def spread_kernel(parts_ref, copies_out):
    total = parts_ref[0].astype(F32)
    for k in range(1, parts_ref.shape[0]):
        total = total + parts_ref[k].astype(F32)
    for k in range(copies_out.shape[0]):
        copies_out[k] = total.astype(BF16)


def unpack_kernel(total_ref, dw1, dw2, dg1, du1, du2, dg2):
    for i in range(LAYERS):
        dw1[i] = total_ref[i, 0:384, :].astype(F32)
        dw2[i] = total_ref[i, 384:512, :].astype(F32)
        du1[i] = total_ref[i, 512:768, :].astype(F32)
        du2[i] = total_ref[i, 768:896, :].astype(F32)
        gains = total_ref[i, 896:912, :].astype(F32)
        dg1[i : i + 1, :] = gains[0:1, :] + gains[8:9, :]
        dg2[i : i + 1, :] = gains[1:2, :] + gains[9:10, :]


def on_device(
    latents,
    edge_latents,
    senders,
    receivers,
    ghost_rows,
    edge_count,
    node_cotangent,
    edge_cotangent,
    edge_first,
    edge_second,
    edge_scale,
    node_first,
    node_second,
    node_scale,
):
    nodes0 = latents[0, 0]
    edges0 = edge_latents[0, 0]
    ids = senders[0]
    targets = receivers[0]
    grow = ghost_rows[0, 0]
    weights = (edge_first, edge_second, edge_scale, node_first, node_second, node_scale)

    node_b = ((NODES, L), BF16)
    node_f = ((NODES, L), F32)
    edge_b = ((EDGES, L), BF16)
    edge_f = ((EDGES, L), F32)
    part_b = ((PART, L), BF16)
    part_f = ((PART, L), F32)
    slabs_b = [((n, G, L), BF16) for n in (3, 3, 2)]
    packed_b = ((PACKED, L), BF16)
    sums_f = ((520, L), F32)
    pair_b = ((NODES, 2 * L), BF16)
    pair_f = ((NODES, 2 * L), F32)
    gain_f = ((8, L), F32)
    dw1_f = ((3 * L, L), F32)
    dw2_f = ((L, L), F32)
    dlocal_f = ((TILE, 2 * L), F32)
    dtile_f = ((TILE, L), F32)

    def before(layer, nodes, edges):
        def part_of(part, wait):
            node_arg = nodes
            if wait is not None:
                node_arg, _ = lax.optimization_barrier((nodes, wait))
            return call(
                functools.partial(before_kernel, part, layer), f"before{layer}{part}",
                [part_b, part_b, part_f], [], 0, 2 * 10**9, node_arg, edges, ids, targets,
                edge_first
            )

        return part_of

    def after(layer, sent, received, edges, z, dy, dz, dsent, edge_grads, sums, partial):
        def part_of(part, wait):
            dy_arg, extra = dy, ()
            if part:
                dy_arg, _ = lax.optimization_barrier((dy, wait[1]))
                extra = (*wait[0][1:], sums, partial)
            outs = [part_b]
            outs += [node_f, packed_b] if part else [dw1_f, dw2_f, dlocal_f, dtile_f]
            return call(
                functools.partial(after_kernel, part, layer), f"after{layer}{part}", outs,
                [dw1_f, dw2_f, dlocal_f, dtile_f] if part else [], 0, 2 * 10**9, sent,
                received[part], edges, z, dy_arg, dz, dsent, ids, targets, edge_first, edge_grads,
                *extra
            )

        return part_of

    picked = call(pick_kernel, "pick", slabs_b, [], 0, 10**8, nodes0, grow)
    ghosts, a0, a1 = exchange(picked, before(0, nodes0, edges0))
    nodes1, inbound, *picked, edges1, sent_0, z_0, n_0, rstd_0 = call(
        first_kernel, "first", [node_b, node_b, *slabs_b, edge_b, edge_b, edge_f, edge_f, edge_f],
        [pair_b, node_f], 1, 4 * 10**9, edge_count, nodes0, edges0, ids, targets, grow, *weights,
        a0[0], a0[2], a1[0], a1[2], *ghosts
    )
    received_0 = (a0[1], a1[1])
    ghosts, a0, a1 = exchange(picked, before(1, nodes1, edges1))
    received_1 = (a0[1], a1[1])
    nodes2, edges2, sent_1, z_1, dy, dz, dsent, partial, sums, *ghost_grad = call(
        middle_kernel, "middle",
        [node_b, edge_b, edge_b, edge_f, edge_b, edge_b, edge_b, node_f, sums_f, *slabs_b],
        [pair_b, node_f, edge_f, edge_f, node_b, pair_f, gain_f], 1, 8 * 10**9, edge_count, nodes1,
        edges1, ids, targets, *weights, node_cotangent[0, 0], edge_cotangent[0, 0], a0[0], a0[2],
        a1[0], a1[2], *ghosts
    )
    returned, c0, c1 = exchange(
        ghost_grad,
        after(1, sent_1, received_1, edges1, z_1, dy, dz, dsent, edge_cotangent[0, 0], sums, partial),
    )
    edge_grad0, (edge_grad1, partial, packed1) = c0[0], c1
    dy, dz, dsent, partial, sums, *ghost_grad = call(
        last_kernel, "last", [edge_b, edge_b, edge_b, node_f, sums_f, *slabs_b],
        [node_b, pair_f, gain_f, edge_b], 1, 4 * 10**9, edge_count, nodes0, inbound, ids, targets,
        grow, *weights, partial, edge_grad0, edge_grad1, z_0, n_0, rstd_0, *returned
    )
    (packed,) = call(
        weights_kernel, "weights", [((LAYERS * PACKED, L), BF16)], [dw1_f, dw2_f], 0, 2 * 10**9,
        sent_0, *received_0, edges0, z_0, dy, dz, sums, packed1
    )
    total, returned, dsent = sum_over_domains(packed, ghost_grad, dsent)
    edge_grad, partial = call(
        shares_kernel, "shares", [edge_f, node_f], [dlocal_f, dtile_f, dtile_f], 0, 2 * 10**9, dz,
        dsent, ids, targets, edge_first, edge_grad0, edge_grad1, partial
    )
    (node_grad,) = call(
        return_kernel, "returned", [node_f], [], 0, 10**8, partial, grow, *returned
    )
    grads = call(
        unpack_kernel, "unpack", [((LAYERS,) + w.shape[1:], F32) for w in weights], [], 0, 10**6,
        total
    )
    return (
        nodes2[None, None],
        edges2[None, None],
        node_grad[None, None],
        edge_grad[None, None],
        *grads,
    )


def solution(mesh):
    domain = P("gx", "gy", None, None)
    placed = (
        domain,
        domain,
        P("gx", "gy", None),
        P("gx", "gy", None),
        P("gx", "gy", None, None, None),
        P("gx", "gy"),
        domain,
        domain,
        P(),
        P(),
        P(),
        P(),
        P(),
        P(),
    )
    return jax.shard_map(
        on_device,
        mesh=mesh,
        in_specs=placed,
        out_specs=(domain, domain, domain, domain, P(), P(), P(), P(), P(), P()),
        check_vma=False,
    )
```

```python
import functools

import jax
import jax.numpy as jnp
from jax import lax
from jax.experimental import pallas as pl
from jax.experimental.pallas import tpu as pltpu
from jax.sharding import PartitionSpec as P

L = 128
LAYERS = 2
TILE = 256
DEG = 8
G = 128
NODES = 512
EDGES = 4096
PART = TILE * DEG
BLOCK = 1024
BLOCKS = EDGES // BLOCK
PART_BLOCKS = PART // BLOCK
PACKED = 1024
OUTER = ((0, 0), (0, 1), (0, 2), (1, 0), (1, 2), (2, 0), (2, 1), (2, 2))

F32 = jnp.float32
BF16 = jnp.bfloat16
epsilon = 1e-05


def dot(a, b):
    return jnp.dot(a, b, preferred_element_type=F32)


def dot_nt(a, b):
    return lax.dot_general(a, b, (((1,), (1,)), ((), ())), preferred_element_type=F32)


def dot_tn(a, b):
    return lax.dot_general(a, b, (((0,), (0,)), ((), ())), preferred_element_type=F32)


def sigmoid(v):
    return 0.5 * jnp.tanh(0.5 * v) + 0.5


def column(row):
    parts = [
        jnp.transpose(jnp.broadcast_to(row[:, i : i + 128], (128, 128)))
        for i in range(0, row.shape[1], 128)
    ]
    return jnp.concatenate(parts, axis=0) if len(parts) > 1 else parts[0]


def hits(col, width):
    lane = lax.broadcasted_iota(jnp.int32, col.shape, 1)
    parts = [
        jnp.where(col == lane + 128 * t, 1.0, 0.0).astype(BF16) for t in range(width // 128)
    ]
    return jnp.concatenate(parts, axis=1)


def hits_t(row, height):
    sub = lax.broadcasted_iota(jnp.int32, (height, row.shape[1]), 0)
    return jnp.where(sub == row, 1.0, 0.0).astype(BF16)


def layer_norm(y):
    center = y - jnp.mean(y, axis=-1, keepdims=True)
    spread = jnp.mean(center * center, axis=-1, keepdims=True)
    rstd = lax.rsqrt(spread + epsilon)
    return center * rstd, rstd


def layer_norm_grad(dn, n, rstd):
    return rstd * (
        dn
        - jnp.mean(dn, axis=-1, keepdims=True)
        - n * jnp.mean(dn * n, axis=-1, keepdims=True)
    )


def silu_grad(z):
    s = sigmoid(z)
    return s * (1.0 + z * (1.0 - s))


def block_at(b):
    return pl.ds(pl.multiple_of(b * BLOCK, BLOCK), BLOCK)


def tile_at(b):
    return pl.ds(pl.multiple_of((b // PART_BLOCKS) * TILE, TILE), TILE)


def index_row(ref, b):
    return ref[:, block_at(b)]


def local_index(ids):
    return jnp.where(ids < TILE, ids, jnp.where(ids < NODES, ids - TILE, -1))


def ghost_index(ids):
    g = ids - NODES
    g = jnp.where(g >= 4 * G, g - G, g)
    return jnp.where(g >= NODES, g - NODES, g)


def ghost_upper(ids):
    return ids >= NODES + NODES + G


def live_of(b, count):
    slot = lax.broadcasted_iota(jnp.int32, (BLOCK, L), 0) + b * BLOCK
    return jnp.where(slot < count, 1.0, 0.0)


def pick(nodes_b, ghost_row_ref, slabs):
    rows = []
    for i, j in OUTER:
        col = column(ghost_row_ref[i, j : j + 1, :])
        rows.append(dot(hits(col, NODES), nodes_b).astype(BF16))
    put_slabs(rows, slabs)


def even_on(axis):
    return lax.rem(lax.axis_index(axis), 2) == 0


def put_slabs(rows, slabs):
    to_even, to_odd, same = slabs
    is_even = even_on("gx")
    for i in range(3):
        to_even[i] = jnp.where(is_even, rows[5 + i], rows[i])
        to_odd[i] = jnp.where(is_even, rows[i], rows[5 + i])
    same[0] = rows[3]
    same[1] = rows[4]


def from_both(is_even, even_ref, odd_ref, i):
    even, odd = even_ref[i], odd_ref[i]
    return jnp.where(is_even, odd, even), jnp.where(is_even, even, odd)


def arrived(refs):
    even_x, odd_x, even_y, odd_y = refs
    row = from_both(even_on("gx"), even_x, odd_x, 1)
    columns = [from_both(even_on("gy"), even_y, odd_y, i) for i in range(3)]
    return [
        columns[0][0], row[0], columns[0][1], columns[1][0], columns[1][1], columns[2][0], row[1],
        columns[2][1]
    ]


def local_pair(nodes_ref):
    return jnp.concatenate([nodes_ref[0:TILE, :], nodes_ref[TILE:NODES, :]], axis=1)


def ghost_pair(ghost_refs):
    rows = arrived(ghost_refs)
    lower = jnp.concatenate(rows[:4], axis=0)
    upper = jnp.concatenate(rows[4:], axis=0)
    return jnp.concatenate([lower, upper], axis=1)


def nodes_forward(nodes_b, inbound_b, u1, u2, gain):
    joined = jnp.concatenate([nodes_b, inbound_b], axis=1)
    z = dot(joined, u1)
    hidden = (z * sigmoid(z)).astype(BF16)
    n, rstd = layer_norm(dot(hidden, u2))
    nodes_next = (nodes_b.astype(F32) + n * gain).astype(BF16)
    return joined, z, hidden, n, rstd, nodes_next


def nodes_backward(grad, joined, z, hidden, n, rstd, u1, u2, gain, sums):
    sums[384:512, :] = dot_tn(hidden, (dy := layer_norm_grad(grad * gain, n, rstd).astype(BF16)))
    sums[513:514, :] = jnp.sum(grad * n, axis=0, keepdims=True)
    dz = (dot_nt(dy, u2).astype(BF16).astype(F32) * silu_grad(z)).astype(BF16)
    sums[128:384, :] = dot_tn(joined, dz)
    back = dot_nt(dz, u1).astype(BF16)
    return back[:, :L].astype(F32), back[:, L:]


def before_kernel(part, layer, nodes_ref, edges_ref, send_ref, recv_ref, w1_ref, sent_out,
                  received_out, z_out):
    pair = local_pair(nodes_ref)
    tile = nodes_ref[part * TILE : (part + 1) * TILE, :]
    w1 = w1_ref[layer]

    def step(i, carry):
        b = i + part * PART_BLOCKS
        ids = index_row(send_ref, b)
        both = dot(hits(column(local_index(ids)), TILE), pair)
        sent = jnp.where(column(ids) >= TILE, both[:, L:], both[:, :L]).astype(BF16)
        received = dot(hits(column(index_row(recv_ref, b)), TILE), tile).astype(BF16)
        sent_out[block_at(i), :] = sent
        received_out[block_at(i), :] = received
        joined = jnp.concatenate([sent, received, edges_ref[block_at(b), :]], axis=1)
        z_out[block_at(i), :] = dot(joined, w1)
        return carry

    lax.fori_loop(0, PART_BLOCKS, step, 0)


def edges_forward(b, local, count, table, edges_ref, send_ref, recv_ref, w1s, w2, gain, inbound,
                  edges_out, sent_out, z_out, n_out, rstd_out):
    sent_ref, z_ref, i = local
    ids = index_row(send_ref, b)
    both = dot(hits(column(ghost_index(ids)), NODES), table)
    sent = jnp.where(column(ids) >= 2 * NODES + G, both[:, L:], both[:, :L]).astype(BF16)
    z = z_ref[block_at(i), :] + dot(sent, w1s)
    hidden = (z * sigmoid(z)).astype(BF16)
    n, rstd = layer_norm(dot(hidden, w2))
    message = n * gain * live_of(b, count)
    at = block_at(b)
    edges_out[at, :] = (edges_ref[at, :].astype(F32) + message).astype(BF16)
    inbound[tile_at(b), :] += dot(hits_t(index_row(recv_ref, b), TILE), message.astype(BF16))
    sent_out[at, :] = sent_ref[block_at(i), :] + sent
    z_out[at, :] = z
    n_out[at, :] = n
    rstd_out[at, :] = jnp.broadcast_to(rstd, (BLOCK, L))


def all_edges_forward(count, locals_, ghost_refs, table, edges_ref, send_ref, recv_ref, w1s, w2,
                      gain, inbound, outs):
    table[...] = ghost_pair(ghost_refs)
    inbound[...] = jnp.zeros_like(inbound)
    for part in range(2):
        sent_ref, z_ref = locals_[2 * part : 2 * part + 2]

        def step(i, carry, part=part, sent_ref=sent_ref, z_ref=z_ref):
            edges_forward(
                i + part * PART_BLOCKS, (sent_ref, z_ref, i), count, table[...], edges_ref,
                send_ref, recv_ref, w1s, w2, gain, inbound, *outs
            )
            return carry

        lax.fori_loop(0, PART_BLOCKS, step, 0, unroll=True)


def edges_backward(b, count, grad_ref, dinbound, z_ref, n_ref, rstd_ref, send_ref, recv_ref, w1s,
                   w2, gain, dy_out, dz_out, dsent_out, gain_sum, dtable):
    at = block_at(b)
    n = n_ref[at, :]
    from_nodes = dot(hits(column(index_row(recv_ref, b)), TILE), dinbound[tile_at(b), :])
    dmessage = (grad_ref[at, :].astype(F32) + from_nodes) * live_of(b, count)
    gain_sum[0:1, :] += jnp.sum(dmessage * n, axis=0, keepdims=True)
    dy = layer_norm_grad(dmessage * gain, n, rstd_ref[at, :]).astype(BF16)
    dz = (dot_nt(dy, w2).astype(BF16).astype(F32) * silu_grad(z_ref[at, :])).astype(BF16)
    dsent = dot_nt(dz, w1s).astype(BF16)
    dy_out[at, :] = dy
    dz_out[at, :] = dz
    dsent_out[at, :] = dsent
    ids = index_row(send_ref, b)
    upper = column(ids) >= 2 * NODES + G
    dsent32 = dsent.astype(F32)
    pair = jnp.concatenate(
        [jnp.where(upper, 0.0, dsent32).astype(BF16), jnp.where(upper, dsent32, 0.0).astype(BF16)],
        axis=1,
    )
    dtable[...] += dot(hits_t(ghost_index(ids), NODES), pair)


def all_edges_backward(count, grad_ref, dinbound, residuals, send_ref, recv_ref, w1s, w2, gain,
                       outs, gain_sum, dtable, ghost_grad_out):
    gain_sum[...] = jnp.zeros_like(gain_sum)
    dtable[...] = jnp.zeros_like(dtable)

    def step(b, carry):
        edges_backward(
            b, count, grad_ref, dinbound, *residuals, send_ref, recv_ref, w1s, w2, gain, *outs,
            gain_sum, dtable
        )
        return carry

    lax.fori_loop(0, BLOCKS, step, 0, unroll=True)
    rows = []
    for s in range(8):
        at, half = pl.ds((s % 4) * G, G), pl.ds((s // 4) * L, L)
        rows.append(dtable[at, half].astype(BF16))
    put_slabs(rows, ghost_grad_out)


def add_weights(b, i, sent_ref, received_ref, edges_ref, z_ref, dy_ref, dz_ref, dw1, dw2):
    at = block_at(b)
    z = z_ref[at, :]
    dw2[...] += dot_tn((z * sigmoid(z)).astype(BF16), dy_ref[at, :])
    joined = jnp.concatenate(
        [sent_ref[at, :], received_ref[block_at(i), :], edges_ref[at, :]], axis=1
    )
    dw1[...] += dot_tn(joined, dz_ref[at, :])


def add_shares(b, dz_ref, dsent_ref, send_ref, recv_ref, w1re, edge_grad, dlocal, dtile):
    at = block_at(b)
    back = dot_nt(dz_ref[at, :], w1re).astype(BF16)
    dtile[...] += dot(hits_t(index_row(recv_ref, b), TILE), back[:, :L])
    ids = index_row(send_ref, b)
    upper = column(ids) >= TILE
    dsent32 = dsent_ref[at, :].astype(F32)
    pair = jnp.concatenate(
        [jnp.where(upper, 0.0, dsent32).astype(BF16), jnp.where(upper, dsent32, 0.0).astype(BF16)],
        axis=1,
    )
    dlocal[...] += dot(hits_t(local_index(ids), TILE), pair)
    return edge_grad + back[:, L:].astype(F32)


def pack(dw1, dw2, sums_ref, packed_out):
    gains = sums_ref[512:520, :]
    high = gains.astype(BF16).astype(F32)
    packed_out[0:384, :] = dw1[...].astype(BF16)
    packed_out[384:512, :] = dw2[...].astype(BF16)
    packed_out[512:896, :] = sums_ref[128:512, :].astype(BF16)
    packed_out[896:912, :] = jnp.concatenate([high, gains - high], axis=0).astype(BF16)
    packed_out[912:PACKED, :] = jnp.zeros((PACKED - 912, L), BF16)


def add_partial(partial_ref, dlocal, dtile0, dtile1, partial_out):
    partial_out[0:TILE, :] = partial_ref[0:TILE, :] + dtile0[...] + dlocal[:, :L]
    partial_out[TILE:, :] = partial_ref[TILE:, :] + dtile1[...] + dlocal[:, L:]


def after_kernel(part, layer, sent_ref, received_ref, edges_ref, z_ref, dy_ref, dz_ref, dsent_ref,
                 send_ref, recv_ref, w1_ref, edge_grad_ref, *rest):
    if part:
        dw1_in, dw2_in, dlocal_in, dtile_in, sums_ref, partial_ref = rest[:6]
        edge_grad_out, partial_out, packed_out, dw1, dw2, dlocal, dtile = rest[6:]
        dw1[...] = dw1_in[...]
        dw2[...] = dw2_in[...]
        dlocal[...] = dlocal_in[...]
    else:
        edge_grad_out, dw1, dw2, dlocal, dtile = rest
        dw1[...] = jnp.zeros_like(dw1)
        dw2[...] = jnp.zeros_like(dw2)
        dlocal[...] = jnp.zeros_like(dlocal)
    dtile[...] = jnp.zeros_like(dtile)
    w1re = w1_ref[layer, L:, :]

    def step(i, carry):
        b = i + part * PART_BLOCKS
        add_weights(b, i, sent_ref, received_ref, edges_ref, z_ref, dy_ref, dz_ref, dw1, dw2)
        grad = edge_grad_ref[block_at(b), :].astype(F32)
        grad = add_shares(b, dz_ref, dsent_ref, send_ref, recv_ref, w1re, grad, dlocal, dtile)
        edge_grad_out[block_at(i), :] = grad.astype(BF16)
        return carry

    lax.fori_loop(0, PART_BLOCKS, step, 0)
    if part:
        add_partial(partial_ref, dlocal, dtile_in, dtile, partial_out)
        pack(dw1, dw2, sums_ref, packed_out)


def weights_kernel(sent_ref, received0, received1, edges_ref, z_ref, dy_ref, dz_ref, sums_ref,
                   packed1_ref, packed_out, dw1, dw2):
    dw1[...] = jnp.zeros_like(dw1)
    dw2[...] = jnp.zeros_like(dw2)
    for part, received_ref in enumerate((received0, received1)):
        for i in range(PART_BLOCKS):
            add_weights(
                i + part * PART_BLOCKS, i, sent_ref, received_ref, edges_ref, z_ref, dy_ref, dz_ref,
                dw1, dw2
            )
    pack(dw1, dw2, sums_ref, packed_out)
    packed_out[PACKED:, :] = packed1_ref[...]


def shares_kernel(dz_ref, dsent_ref, send_ref, recv_ref, w1_ref, edge_grad0, edge_grad1,
                  partial_ref, edge_grad_out, partial_out, dlocal, dtile0, dtile1):
    dlocal[...] = jnp.zeros_like(dlocal)
    w1re = w1_ref[0, L:, :]
    for part, (edge_grad_ref, dtile) in enumerate(((edge_grad0, dtile0), (edge_grad1, dtile1))):
        dtile[...] = jnp.zeros_like(dtile)

        def step(i, carry, part=part, edge_grad_ref=edge_grad_ref, dtile=dtile):
            b = i + part * PART_BLOCKS
            edge_grad_out[block_at(b), :] = add_shares(
                b, dz_ref, dsent_ref, send_ref, recv_ref, w1re,
                edge_grad_ref[block_at(i), :].astype(F32), dlocal, dtile
            )
            return carry

        lax.fori_loop(0, PART_BLOCKS, step, 0)
    add_partial(partial_ref, dlocal, dtile0, dtile1, partial_out)


def pick_kernel(nodes_ref, ghost_row_ref, *slabs):
    pick(nodes_ref[...], ghost_row_ref, slabs)


def turn_kernel(even_x, odd_x, same, to_even, to_odd):
    rows = [from_both(even_on("gx"), even_x, odd_x, i) for i in (0, 2)]
    is_even = even_on("gy")
    left = (rows[0][0], same[0], rows[0][1])
    right = (rows[1][0], same[1], rows[1][1])
    for i in range(3):
        to_even[i] = jnp.where(is_even, right[i], left[i])
        to_odd[i] = jnp.where(is_even, left[i], right[i])


def first_kernel(
    count_ref, nodes_ref, edges_ref, send_ref, recv_ref, ghost_row_ref, w1_ref, w2_ref, g1_ref,
    u1_ref, u2_ref, g2_ref, sent0, z0, sent1, z1, *rest
):
    ghost_refs, rest = rest[:4], rest[4:]
    nodes_out, inbound_out, *slabs = rest[:5]
    outs, (table, inbound) = rest[5:10], rest[10:]
    all_edges_forward(
        count_ref[0, 0], (sent0, z0, sent1, z1), ghost_refs, table, edges_ref, send_ref, recv_ref,
        w1_ref[0, :L, :], w2_ref[0], g1_ref[0:1, :], inbound, outs
    )
    inbound_b = inbound[...].astype(BF16)
    inbound_out[...] = inbound_b
    nodes_next = nodes_forward(nodes_ref[...], inbound_b, u1_ref[0], u2_ref[0], g2_ref[0:1, :])[-1]
    nodes_out[...] = nodes_next
    pick(nodes_next, ghost_row_ref, slabs)


def start_nodes_backward(grad, nodes_b, inbound_b, layer, u1_ref, u2_ref, g2_ref, sums):
    u1, u2, gain = u1_ref[layer], u2_ref[layer], g2_ref[layer : layer + 1, :]
    sums[512:520, :] = jnp.zeros((8, L), F32)
    *saved, nodes_next = nodes_forward(nodes_b, inbound_b, u1, u2, gain)
    through, dinbound = nodes_backward(grad, *saved, u1, u2, gain, sums)
    return nodes_next, grad + through, dinbound


def middle_kernel(
    count_ref, nodes_ref, edges_ref, send_ref, recv_ref, w1_ref, w2_ref, g1_ref, u1_ref, u2_ref,
    g2_ref, node_grad_ref, edge_grad_ref, sent0, z0, sent1, z1, *rest
):
    ghost_refs, rest = rest[:4], rest[4:]
    nodes_out, edges_out, sent_out, z_out, dy_out, dz_out, dsent_out = rest[:7]
    partial_out, sums, *ghost_grad_out = rest[7:12]
    table, inbound, n_all, rstd_all, dinbound, dtable, gain_sum = rest[12:]
    count = count_ref[0, 0]
    w1s, w2, gain = w1_ref[1, :L, :], w2_ref[1], g1_ref[1:2, :]
    all_edges_forward(
        count, (sent0, z0, sent1, z1), ghost_refs, table, edges_ref, send_ref, recv_ref, w1s, w2,
        gain, inbound, (edges_out, sent_out, z_out, n_all, rstd_all)
    )
    nodes_out[...], partial_out[...], dinbound[...] = start_nodes_backward(
        node_grad_ref[...].astype(F32), nodes_ref[...], inbound[...].astype(BF16), 1, u1_ref,
        u2_ref, g2_ref, sums
    )
    all_edges_backward(
        count, edge_grad_ref, dinbound, (z_out, n_all, rstd_all), send_ref, recv_ref, w1s, w2, gain,
        (dy_out, dz_out, dsent_out), gain_sum, dtable, ghost_grad_out
    )
    sums[512:513, :] = gain_sum[0:1, :]


def last_kernel(
    count_ref, nodes_ref, inbound_ref, send_ref, recv_ref, ghost_row_ref, w1_ref, w2_ref, g1_ref,
    u1_ref, u2_ref, g2_ref, partial_ref, edge_grad0_ref, edge_grad1_ref, z_ref, n_ref, rstd_ref,
    *rest
):
    returned_refs, rest = rest[:4], rest[4:]
    dy_out, dz_out, dsent_out, partial_out, sums, *ghost_grad_out = rest[:8]
    dinbound, dtable, gain_sum, edge_grad = rest[8:]
    node_grad = add_returned(partial_ref[...], returned_refs, ghost_row_ref)
    _, partial_out[...], dinbound[...] = start_nodes_backward(
        node_grad.astype(BF16).astype(F32), nodes_ref[...], inbound_ref[...], 0, u1_ref, u2_ref,
        g2_ref, sums
    )
    edge_grad[0:PART, :] = edge_grad0_ref[...]
    edge_grad[PART:, :] = edge_grad1_ref[...]
    all_edges_backward(
        count_ref[0, 0], edge_grad, dinbound, (z_ref, n_ref, rstd_ref), send_ref, recv_ref,
        w1_ref[0, :L, :], w2_ref[0], g1_ref[0:1, :], (dy_out, dz_out, dsent_out), gain_sum, dtable,
        ghost_grad_out
    )
    sums[512:513, :] = gain_sum[0:1, :]


def add_returned(partial, returned_refs, ghost_row_ref):
    row = jnp.concatenate([ghost_row_ref[i, j : j + 1, :] for i, j in OUTER], axis=1)
    returned = jnp.concatenate(arrived(returned_refs), axis=0)
    return partial + dot(hits_t(row, NODES), returned)


def return_kernel(partial_ref, ghost_row_ref, *rest):
    rest[4][...] = add_returned(partial_ref[...], rest[:4], ghost_row_ref)


def call(kernel, name, outs, scratch, scalars, flops, *args):
    vmem = pl.BlockSpec(memory_space=pltpu.VMEM)
    smem = pl.BlockSpec(memory_space=pltpu.SMEM)
    return pl.pallas_call(
        kernel,
        name=name,
        out_shape=[jax.ShapeDtypeStruct(s, d) for s, d in outs],
        in_specs=[smem] * scalars + [vmem] * (len(args) - scalars),
        out_specs=[vmem] * len(outs),
        scratch_shapes=[pltpu.VMEM(s, d) for s, d in scratch],
        cost_estimate=pl.CostEstimate(flops=flops, bytes_accessed=1 << 20, transcendentals=0),
        compiler_params=pltpu.CompilerParams(vmem_limit_bytes=24 * 1024 * 1024),
    )(*args)


def swap(axis, to_even, to_odd):
    def pairs(first):
        ups = [(i, i + 1) for i in range(first, lax.axis_size(axis) - 1, 2)]
        return ups + [(j, i) for i, j in ups]

    odd = lax.ppermute(to_odd, axis, pairs(1))
    return lax.ppermute(to_even, axis, pairs(0)), odd


def turn(even_x, odd_x, same):
    outs = [(even_x.shape, BF16)] * 2
    return call(turn_kernel, "turn", outs, [], 0, 10**6, even_x, odd_x, same)


def exchange(slabs, beside):
    to_even, to_odd, same = slabs
    even_x, odd_x = swap("gx", to_even, to_odd)
    first = beside(0, None)
    to_even, to_odd = turn(even_x, odd_x, same)
    even_y, odd_y = swap("gy", to_even, to_odd)
    second = beside(1, (first, to_even))
    return (even_x, odd_x, even_y, odd_y), first, second


def sum_over_domains(packed, slabs, late):
    axes = ("gx", "gy")
    plane, line = planes_and_lines(lax.axis_size("gx"), lax.axis_size("gy"))
    hold = lax.optimization_barrier

    def trade(parts, groups):
        return lax.all_to_all(parts, axes, 0, 0, tiled=True, axis_index_groups=groups)

    def copies(parts, groups):
        shape = (len(groups[0]),) + parts.shape[1:]
        return call(spread_kernel, "spread", [(shape, BF16)], [], 0, 10**6, parts)[0]

    to_even, to_odd, same = slabs
    packed, to_even, to_odd = hold((packed.reshape(len(plane[0]), -1, L), to_even, to_odd))
    parts = trade(packed, plane)
    parts, even_x, odd_x = hold((parts, *swap("gx", to_even, to_odd)))
    parts, same = hold((copies(parts, line), same))
    parts = trade(parts, line)
    parts, even_y, odd_y = hold((parts, *swap("gy", *turn(even_x, odd_x, same))))
    parts, late = hold((copies(parts, plane), late))
    total = trade(parts, plane).reshape(LAYERS, PACKED, L)
    return total, (even_x, odd_x, even_y, odd_y), late


def planes_and_lines(rows, columns):
    planes, lines = {}, {}
    for i in range(rows * columns):
        gx, gy = divmod(i, columns)
        y, z_low = divmod(gx, 4)
        z_high, rest = divmod(gy, 8)
        planes.setdefault((z_high, z_low), []).append(i)
        lines.setdefault((y, rest), []).append(i)
    return list(planes.values()), list(lines.values())


def spread_kernel(parts_ref, copies_out):
    total = parts_ref[0].astype(F32)
    for k in range(1, parts_ref.shape[0]):
        total = total + parts_ref[k].astype(F32)
    for k in range(copies_out.shape[0]):
        copies_out[k] = total.astype(BF16)


def unpack_kernel(total_ref, dw1, dw2, dg1, du1, du2, dg2):
    for i in range(LAYERS):
        dw1[i] = total_ref[i, 0:384, :].astype(F32)
        dw2[i] = total_ref[i, 384:512, :].astype(F32)
        du1[i] = total_ref[i, 512:768, :].astype(F32)
        du2[i] = total_ref[i, 768:896, :].astype(F32)
        gains = total_ref[i, 896:912, :].astype(F32)
        dg1[i : i + 1, :] = gains[0:1, :] + gains[8:9, :]
        dg2[i : i + 1, :] = gains[1:2, :] + gains[9:10, :]


def on_device(
    latents,
    edge_latents,
    senders,
    receivers,
    ghost_rows,
    edge_count,
    node_cotangent,
    edge_cotangent,
    edge_first,
    edge_second,
    edge_scale,
    node_first,
    node_second,
    node_scale,
):
    nodes0 = latents[0, 0]
    edges0 = edge_latents[0, 0]
    ids = senders[0]
    targets = receivers[0]
    grow = ghost_rows[0, 0]
    weights = (edge_first, edge_second, edge_scale, node_first, node_second, node_scale)

    node_b = ((NODES, L), BF16)
    node_f = ((NODES, L), F32)
    edge_b = ((EDGES, L), BF16)
    edge_f = ((EDGES, L), F32)
    part_b = ((PART, L), BF16)
    part_f = ((PART, L), F32)
    slabs_b = [((n, G, L), BF16) for n in (3, 3, 2)]
    packed_b = ((PACKED, L), BF16)
    sums_f = ((520, L), F32)
    pair_b = ((NODES, 2 * L), BF16)
    pair_f = ((NODES, 2 * L), F32)
    gain_f = ((8, L), F32)
    dw1_f = ((3 * L, L), F32)
    dw2_f = ((L, L), F32)
    dlocal_f = ((TILE, 2 * L), F32)
    dtile_f = ((TILE, L), F32)

    def before(layer, nodes, edges):
        def part_of(part, wait):
            node_arg = nodes
            if wait is not None:
                node_arg, _ = lax.optimization_barrier((nodes, wait))
            return call(
                functools.partial(before_kernel, part, layer), f"before{layer}{part}",
                [part_b, part_b, part_f], [], 0, 2 * 10**9, node_arg, edges, ids, targets,
                edge_first
            )

        return part_of

    def after(layer, sent, received, edges, z, dy, dz, dsent, edge_grads, sums, partial):
        def part_of(part, wait):
            dy_arg, extra = dy, ()
            if part:
                dy_arg, _ = lax.optimization_barrier((dy, wait[1]))
                extra = (*wait[0][1:], sums, partial)
            outs = [part_b]
            outs += [node_f, packed_b] if part else [dw1_f, dw2_f, dlocal_f, dtile_f]
            return call(
                functools.partial(after_kernel, part, layer), f"after{layer}{part}", outs,
                [dw1_f, dw2_f, dlocal_f, dtile_f] if part else [], 0, 2 * 10**9, sent,
                received[part], edges, z, dy_arg, dz, dsent, ids, targets, edge_first, edge_grads,
                *extra
            )

        return part_of

    picked = call(pick_kernel, "pick", slabs_b, [], 0, 10**8, nodes0, grow)
    ghosts, a0, a1 = exchange(picked, before(0, nodes0, edges0))
    nodes1, inbound, *picked, edges1, sent_0, z_0, n_0, rstd_0 = call(
        first_kernel, "first", [node_b, node_b, *slabs_b, edge_b, edge_b, edge_f, edge_f, edge_f],
        [pair_b, node_f], 1, 4 * 10**9, edge_count, nodes0, edges0, ids, targets, grow, *weights,
        a0[0], a0[2], a1[0], a1[2], *ghosts
    )
    received_0 = (a0[1], a1[1])
    ghosts, a0, a1 = exchange(picked, before(1, nodes1, edges1))
    received_1 = (a0[1], a1[1])
    nodes2, edges2, sent_1, z_1, dy, dz, dsent, partial, sums, *ghost_grad = call(
        middle_kernel, "middle",
        [node_b, edge_b, edge_b, edge_f, edge_b, edge_b, edge_b, node_f, sums_f, *slabs_b],
        [pair_b, node_f, edge_f, edge_f, node_b, pair_f, gain_f], 1, 8 * 10**9, edge_count, nodes1,
        edges1, ids, targets, *weights, node_cotangent[0, 0], edge_cotangent[0, 0], a0[0], a0[2],
        a1[0], a1[2], *ghosts
    )
    returned, c0, c1 = exchange(
        ghost_grad,
        after(1, sent_1, received_1, edges1, z_1, dy, dz, dsent, edge_cotangent[0, 0], sums, partial),
    )
    edge_grad0, (edge_grad1, partial, packed1) = c0[0], c1
    dy, dz, dsent, partial, sums, *ghost_grad = call(
        last_kernel, "last", [edge_b, edge_b, edge_b, node_f, sums_f, *slabs_b],
        [node_b, pair_f, gain_f, edge_b], 1, 4 * 10**9, edge_count, nodes0, inbound, ids, targets,
        grow, *weights, partial, edge_grad0, edge_grad1, z_0, n_0, rstd_0, *returned
    )
    (packed,) = call(
        weights_kernel, "weights", [((LAYERS * PACKED, L), BF16)], [dw1_f, dw2_f], 0, 2 * 10**9,
        sent_0, *received_0, edges0, z_0, dy, dz, sums, packed1
    )
    total, returned, held_ids = sum_over_domains(packed, ghost_grad, ids)
    edge_grad, partial = call(
        shares_kernel, "shares", [edge_f, node_f], [dlocal_f, dtile_f, dtile_f], 0, 2 * 10**9, dz,
        dsent, held_ids, targets, edge_first, edge_grad0, edge_grad1, partial
    )
    (node_grad,) = call(
        return_kernel, "returned", [node_f], [], 0, 10**8, partial, grow, *returned
    )
    grads = call(
        unpack_kernel, "unpack", [((LAYERS,) + w.shape[1:], F32) for w in weights], [], 0, 10**6,
        total
    )
    return (
        nodes2[None, None],
        edges2[None, None],
        node_grad[None, None],
        edge_grad[None, None],
        *grads,
    )


def solution(mesh):
    domain = P("gx", "gy", None, None)
    placed = (
        domain,
        domain,
        P("gx", "gy", None),
        P("gx", "gy", None),
        P("gx", "gy", None, None, None),
        P("gx", "gy"),
        domain,
        domain,
        P(),
        P(),
        P(),
        P(),
        P(),
        P(),
    )
    return jax.shard_map(
        on_device,
        mesh=mesh,
        in_specs=placed,
        out_specs=(domain, domain, domain, domain, P(), P(), P(), P(), P(), P()),
        check_vma=False,
    )
```
